128 devices in a mesh: scen: 4 (over z_hi, core), trade: 32 (over z_lo, x, y).
Axes of the slice: x: 4, y: 4, z: 4 (z_hi: 2, z_lo: 2; z = z_hi * 2 + z_lo), core: 2. Of those that a mesh axis runs over, the one named last changes fastest.
Arguments:
- normal_draws: bfloat16 [2, 2048, 4096], P(None, 'scen', 'trade'), may hold values from -6 to 6
- covariance_root: bfloat16 [4096, 4096], P('trade'), as said below
- mean_pullback: float32 [4096], replicated, may hold values from 0.3 to 0.97
- sensitivity_tensor: bfloat16 [4096, 65536], P(None, 'trade'), may hold values from -0.09375 to 0.09375
- moneyness_shift: float32 [65536], P('trade'), may hold values from -5 to 5
- signed_principal: float32 [65536], P('trade'), may hold values from -1 to 1
- deal_agreement_group: int32 [65536], P('trade'), may hold values from 0 to 511
- active_position_number: int32 [32], P('trade'), may hold values from 512 to 2048, as said below
Outputs:
- exposure: float32 [2, 2048, 512], P(None, 'scen', 'trade')
- expected_exposure: float32 [2, 512], P(None, 'trade')
The draws below stay inside these ranges and needn't reach their ends.
Inputs may be any that keep to these rules, and one draw needn't show every extreme that they name: Each trade shard's first active_position_number slots hold trades, the rest are empty; some shard holds 2048 live trades in every draw. `covariance_root`: upper triangular with a positive diagonal.
All inputs are finite; a program needn't handle non-finite values.
Results may differ from the reference program's by a relative error of at most 0.0034.
Values may be sent and summed in bfloat16 or wider, within the bound.
A program may use at most 128 MiB of HBM per device.

```python
import math
import jax
import jax.numpy as jnp
from jax import lax

RISK_DRIVERS = 4096
PIECE_POSITIONS = 2048
SETS_DEV = 16
DATES = 2
SCEN = 2048
DEAL_POSITIONS = 65536
NSETS = 512
N_TRADE = 32


def draw_covariance_root(key, part):
    key = jax.random.fold_in(key, 11)
    key_off = jax.random.fold_in(key, 1)
    key_diag = jax.random.fold_in(key, 2)
    spread = jax.random.normal(key_off, (RISK_DRIVERS, RISK_DRIVERS), jnp.float32)
    spread = spread / jnp.sqrt(jnp.float32(RISK_DRIVERS))
    diagonal = jax.random.uniform(key_diag, (RISK_DRIVERS,), jnp.float32, 0.5, 1.0)
    row_ids = jnp.arange(RISK_DRIVERS, dtype=jnp.int32)[:, None]
    col_ids = jnp.arange(RISK_DRIVERS, dtype=jnp.int32)[None, :]
    upper = jnp.where(col_ids > row_ids, spread, 0.0)
    upper = jnp.where(col_ids == row_ids, diagonal[:, None] * jnp.ones((1, RISK_DRIVERS), jnp.float32), upper)
    return upper.astype(jnp.bfloat16)


def draw_active_position_number(key, part):
    key = jax.random.fold_in(key, 12)
    key_count = jax.random.fold_in(key, 1)
    key_full = jax.random.fold_in(key, 2)
    counts = jax.random.randint(key_count, (N_TRADE,), PIECE_POSITIONS // 4, PIECE_POSITIONS + 1, jnp.int32)
    full_shard = jax.random.randint(key_full, (), 0, N_TRADE, jnp.int32)
    return jnp.where(jnp.arange(N_TRADE, dtype=jnp.int32) == full_shard, PIECE_POSITIONS, counts).astype(jnp.int32)


def set_ends(result, own_key, low, largest):
    dims = result.shape
    index_at = [jax.random.randint(jax.random.fold_in(own_key, axis), (), 0, dims[axis]) for axis in range(len(dims))]
    result = result.at[tuple(index_at)].set(low)
    longest = dims.index(max(dims))
    index_at[longest] = (index_at[longest] + 1) % dims[longest]
    return result.at[tuple(index_at)].set(largest)


def shard_levels(stream_key, extent, cuts, smallest, largest):
    def one(axis_at, shards_of):
        draws = jax.random.uniform(jax.random.fold_in(jax.random.fold_in(stream_key, 6), axis_at), (shards_of,), jnp.float32, smallest / len(cuts), largest / len(cuts))
        return jnp.repeat(jnp.exp(draws), extent[axis_at] // shards_of).reshape((-1,) + (1,) * (len(extent) - axis_at - 1))

    factor_of = one(*cuts[0])
    for cut in cuts[1:]:
        factor_of = factor_of * one(*cut)
    return factor_of


def scatter_about(key, shape, scale, limit, cuts=(), kind=jnp.bfloat16):
    drawn = jax.random.normal(key, shape, jnp.float32) * scale
    if len(cuts) > 0:
        drawn = shard_levels(key, shape, cuts, -0.22, 0.18) * drawn
    return jnp.clip(drawn, min=-limit, max=limit).astype(kind)


def setup_inputs(seed: int = 0) -> dict:
    arg_keys = jax.random.split(jax.random.key(seed), 9)
    return {
        "normal_draws": scatter_about(arg_keys[0], (DATES, SCEN, RISK_DRIVERS), 1.0, 6.0, ((1, 4), (2, 32))),
        "covariance_root": draw_covariance_root(jax.random.fold_in(arg_keys[8], 71), 0),
        "mean_pullback": jnp.clip(jnp.exp(jax.random.uniform(arg_keys[2], (RISK_DRIVERS,), jnp.float32, math.log(0.3), math.log(0.97))), 0.3, 0.97),
        "sensitivity_tensor": scatter_about(arg_keys[3], (RISK_DRIVERS, DEAL_POSITIONS), RISK_DRIVERS ** -0.5, 0.09375, ((1, 32),)),
        "moneyness_shift": scatter_about(arg_keys[4], (DEAL_POSITIONS,), 1.0, 5.0, ((0, 32),), jnp.float32),
        "signed_principal": scatter_about(arg_keys[5], (DEAL_POSITIONS,), 0.15, 1.0, ((0, 32),), jnp.float32),
        "deal_agreement_group": set_ends(jax.random.randint(arg_keys[6], (DEAL_POSITIONS,), 0, NSETS), jax.random.fold_in(arg_keys[6], 1), 0, NSETS - 1).astype(jnp.int32),
        "active_position_number": draw_active_position_number(jax.random.fold_in(arg_keys[8], 71), 0),
    }


def reference(normal_draws, covariance_root, mean_pullback, sensitivity_tensor, moneyness_shift, signed_principal, deal_agreement_group, active_position_number):
    slot_index = jnp.arange(DEAL_POSITIONS, dtype=jnp.int32) % PIECE_POSITIONS
    shard_index = jnp.arange(DEAL_POSITIONS, dtype=jnp.int32) // PIECE_POSITIONS
    weight = jnp.where(slot_index < active_position_number[shard_index], signed_principal, jnp.zeros_like(signed_principal))
    set_total = SETS_DEV * N_TRADE
    labels = jnp.arange(set_total, dtype=jnp.int32)
    piece_deal_prices = sensitivity_tensor.reshape(RISK_DRIVERS, N_TRADE, PIECE_POSITIONS).transpose(1, 0, 2)
    shard_strike = moneyness_shift.reshape(N_TRADE, PIECE_POSITIONS)
    shard_weight = weight.reshape(N_TRADE, PIECE_POSITIONS)
    shard_sets = deal_agreement_group.reshape(N_TRADE, PIECE_POSITIONS)
    factor_state = jnp.zeros((SCEN, RISK_DRIVERS), jnp.float32)
    exposures = []
    for date_index in range(DATES):
        factor_state = mean_pullback * factor_state + jnp.dot(normal_draws[date_index], covariance_root, preferred_element_type=jnp.float32)
        levels = factor_state.astype(jnp.bfloat16)

        def shard_net(running, pieces):
            prices, strikes, weights, set_ids = pieces
            moneyness = jnp.dot(levels, prices, preferred_element_type=jnp.float32) + strikes
            values = (weights * jax.nn.softplus(moneyness)).astype(jnp.bfloat16)
            member = (set_ids[:, None] == labels[None, :]).astype(jnp.bfloat16)
            return running + jnp.dot(values, member, preferred_element_type=jnp.float32), None

        net_sum, _ = lax.scan(shard_net, jnp.zeros((SCEN, set_total), jnp.float32), (piece_deal_prices, shard_strike, shard_weight, shard_sets))
        exposures.append(jnp.maximum(net_sum, 0.0))
    exposure = jnp.stack(exposures, 0)
    return exposure, jnp.sum(exposure, axis=1) / SCEN
```

```python
import functools
import jax
import jax.numpy as jnp
from jax import lax
from jax.experimental import pallas as pl
from jax.experimental.pallas import tpu as pltpu
from jax.sharding import PartitionSpec as P

F32, BF16 = jnp.float32, jnp.bfloat16
SETS_DEV = 16
NZ, NX, NY = 2, 4, 4
N_TRADE = NZ * NX * NY
CHUNKS = 4
COLS = 4
ROWS = 64
LANES = 128
TILE = 256
PARTS = (
    ((0, 3), (0, 32), ("z", "y", "x")),
    ((0, 3), (32, 32), ("z", "x", "y")),
    ((3, 1), (0, 64), ("x", "y", "z")),
)
STEPS = 5


def trade_place():
    me = lax.axis_index("trade")
    return {"z": me // (NX * NY), "x": (me // NY) % NX, "y": me % NY}


def trade_index(place):
    return (place["z"] * NX + place["x"]) * NY + place["y"]


def moved(place, axis, by):
    size = {"z": NZ, "x": NX, "y": NY}[axis]
    return dict(place, **{axis: (place[axis] + by) % size})


def part_steps(place, order):
    have = dict(place)
    steps = []
    for axis in order:
        if axis == "z":
            steps.append(
                (
                    [(dict(have), None, moved(place, "z", 1))],
                    [(dict(have, z=1 - place["z"]), None)],
                )
            )
        else:
            right, left = moved(place, axis, 1), moved(place, axis, 3)
            far = moved(place, axis, 2)
            at = lambda where: dict(have, **{axis: where[axis]})
            steps.append(
                (
                    [(at(place), None, right), (at(place), None, left)],
                    [(at(left), None), (at(right), None)],
                )
            )
            steps.append(
                (
                    [(at(left), 0, right), (at(right), 1, left)],
                    [(at(far), 0), (at(far), 1)],
                )
            )
        have[axis] = None
    return steps


def softplus(a):
    return jnp.maximum(a, 0.0) + jnp.log1p(jnp.exp(-jnp.abs(a)))


def value_kernel(
    lev_hbm, sens_hbm, shift_ref, principal_ref, group_ref, live_ref, out_ref,
    book, sens, member, weight, net, net_out, net_in,
    send_sems, recv_sems, own_sem, sens_sem, net_send_sem, net_recv_sems,
):
    place = trade_place()
    me = trade_index(place)
    positions = sens.shape[1]
    sets = member.shape[0]

    fetch = pltpu.make_async_copy(sens_hbm, sens, sens_sem)
    fetch.start()
    own = pltpu.make_async_copy(
        lev_hbm, book.at[:, place["z"], place["x"], :, place["y"]], own_sem
    )
    own.start()

    barrier = pltpu.get_barrier_semaphore()

    @pl.loop(1, N_TRADE)
    def _(step):
        pl.semaphore_signal(
            barrier, inc=1, device_id={"trade": (me + step) % N_TRADE},
            device_id_type=pl.DeviceIdType.MESH,
        )

    pl.semaphore_wait(barrier, N_TRADE - 1)
    own.wait()

    plans = [part_steps(place, order) for _, _, order in PARTS]

    def view(part, chunk, coords, half):
        (col, cols), (row, rows), _ = PARTS[part]
        if half is not None:
            rows = rows // 2
            row = row + half * rows
        pick = [slice(None) if coords[a] is None else coords[a] for a in "zxy"]
        return book.at[chunk, pick[0], pick[1], pl.ds(col, cols), pick[2], pl.ds(row, rows), :]

    def descriptors(part, step, chunk, kind):
        sends, recvs = plans[part][step]
        for way in range(len(sends)):
            if kind == "send":
                coords, half, target = sends[way]
            else:
                coords, half = recvs[way]
                target = place
            ref = view(part, chunk, coords, half)
            yield pltpu.make_async_remote_copy(
                src_ref=ref, dst_ref=ref,
                send_sem=send_sems.at[chunk, part, step, way],
                recv_sem=recv_sems.at[chunk, part, step, way],
                device_id={"trade": trade_index(target)},
                device_id_type=pl.DeviceIdType.MESH,
            )

    def start(step, chunk):
        for part in range(len(PARTS)):
            for copy in descriptors(part, step, chunk, "send"):
                copy.start()

    def arrived(step, chunk):
        for part in range(len(PARTS)):
            for copy in descriptors(part, step, chunk, "recv"):
                copy.wait_recv()

    @pl.loop(0, CHUNKS)
    def _(chunk):
        start(0, chunk)

    weight[...] = jnp.where(
        lax.broadcasted_iota(jnp.int32, (1, positions), 1) < live_ref[...],
        principal_ref[...], 0.0,
    )
    @pl.loop(0, positions // TILE)
    def _(tile):
        at = pl.ds(pl.multiple_of(tile * TILE, TILE), TILE)
        labels = lax.broadcasted_iota(jnp.int32, (sets, TILE), 0)
        member[:, at] = (labels == group_ref[:, at]).astype(F32).astype(BF16)

    for step in (1, 2):
        @pl.loop(0, CHUNKS)
        def _(chunk, step=step):
            arrived(step - 1, chunk)
            start(step, chunk)

    fetch.wait()

    def net_copy(chunk, target):
        return pltpu.make_async_remote_copy(
            src_ref=net_out.at[chunk, target], dst_ref=net_in.at[chunk, me],
            send_sem=net_send_sem, recv_sem=net_recv_sems.at[chunk],
            device_id={"trade": target}, device_id_type=pl.DeviceIdType.MESH,
        )

    def compute(chunk):
        net[...] = jnp.zeros_like(net)
        levels = jnp.concatenate(
            [
                book[chunk, z, x, col].reshape(NY * ROWS, LANES)
                for z in range(NZ) for x in range(NX) for col in range(COLS)
            ],
            axis=1,
        )

        @pl.loop(0, positions // TILE)
        def _(tile):
            at = pl.ds(pl.multiple_of(tile * TILE, TILE), TILE)
            moneyness = jnp.dot(levels, sens[:, at], preferred_element_type=F32)
            values = weight[:, at] * softplus(moneyness + shift_ref[:, at])
            net[...] += lax.dot_general(
                member[:, at], values.astype(BF16), (((1,), (1,)), ((), ())),
                preferred_element_type=F32,
            )

        net_out[chunk] = net[...].astype(BF16).reshape(N_TRADE, SETS_DEV, NY * ROWS)

        @pl.loop(1, N_TRADE)
        def _(step):
            net_copy(chunk, (me + step) % N_TRADE).start()

        net_in[chunk, me] = net_out[chunk, me]

    @pl.loop(0, CHUNKS + 2)
    def _(tick):
        @pl.when(tick < CHUNKS)
        def _():
            arrived(2, tick)
            start(3, tick)

        @pl.when(jnp.logical_and(tick >= 1, tick < CHUNKS + 1))
        def _():
            arrived(3, tick - 1)
            start(4, tick - 1)

        @pl.when(tick >= 2)
        def _():
            arrived(4, tick - 2)
            compute(tick - 2)

    @pl.loop(0, CHUNKS)
    def _(chunk):
        for part in range(len(PARTS)):
            for step in range(STEPS):
                for copy in descriptors(part, step, chunk, "send"):
                    copy.wait_send()

        whole = pltpu.make_async_remote_copy(
            src_ref=net_out.at[chunk, pl.ds(0, N_TRADE - 1)],
            dst_ref=net_in.at[chunk, pl.ds(0, N_TRADE - 1)],
            send_sem=net_send_sem, recv_sem=net_recv_sems.at[chunk],
            device_id={"trade": me}, device_id_type=pl.DeviceIdType.MESH,
        )
        whole.wait_send()
        whole.wait_recv()
        total = jnp.zeros((SETS_DEV, NY * ROWS), F32)
        for sender in range(N_TRADE):
            total = total + net_in[chunk, sender].astype(F32)
        out_ref[chunk] = jnp.maximum(total, 0.0)


def values_and_nets(levels, sensitivity, shift, principal, group, live):
    positions = sensitivity.shape[1]
    sets = SETS_DEV * N_TRADE
    vmem = pl.BlockSpec(memory_space=pltpu.VMEM)
    hbm = pl.BlockSpec(memory_space=pl.ANY)
    return pl.pallas_call(
        value_kernel,
        out_shape=jax.ShapeDtypeStruct((CHUNKS, SETS_DEV, NY * ROWS), F32),
        in_specs=[hbm, hbm, vmem, vmem, vmem, vmem],
        out_specs=vmem,
        scratch_shapes=[
            pltpu.VMEM((CHUNKS, NZ, NX, COLS, NY, ROWS, LANES), BF16),
            pltpu.VMEM(sensitivity.shape, BF16),
            pltpu.VMEM((sets, positions), BF16),
            pltpu.VMEM((1, positions), F32),
            pltpu.VMEM((sets, NY * ROWS), F32),
            pltpu.VMEM((CHUNKS, N_TRADE, SETS_DEV, NY * ROWS), BF16),
            pltpu.VMEM((CHUNKS, N_TRADE, SETS_DEV, NY * ROWS), BF16),
            pltpu.SemaphoreType.DMA((CHUNKS, len(PARTS), STEPS, 2)),
            pltpu.SemaphoreType.DMA((CHUNKS, len(PARTS), STEPS, 2)),
            pltpu.SemaphoreType.DMA,
            pltpu.SemaphoreType.DMA,
            pltpu.SemaphoreType.DMA,
            pltpu.SemaphoreType.DMA((CHUNKS,)),
        ],
        compiler_params=pltpu.CompilerParams(
            collective_id=1, has_side_effects=True, vmem_limit_bytes=58 * 2**20
        ),
        cost_estimate=pl.CostEstimate(
            flops=2 * 1024 * positions * (4096 + sets), bytes_accessed=17 << 20, transcendentals=0
        ),
        name="value_nets",
    )(
        levels, sensitivity, shift.reshape(1, -1), principal.reshape(1, -1),
        group.reshape(1, -1), live.reshape(1, 1),
    )


def on_device(
    normal_draws, covariance_root, mean_pullback, sensitivity_tensor,
    moneyness_shift, signed_principal, deal_agreement_group, active_position_number,
):
    dates, scen = normal_draws.shape[:2]
    span = scen // NY // CHUNKS
    partial = jnp.dot(normal_draws, covariance_root, preferred_element_type=F32)
    partial = partial.reshape(dates, NY, CHUNKS, span, NZ * NX, COLS, LANES)
    partial = partial.transpose(4, 1, 2, 5, 0, 3, 6)
    partial = partial.reshape(N_TRADE, CHUNKS, COLS, dates, span, LANES)
    shocks = lax.psum_scatter(partial, "trade", scatter_dimension=0, tiled=False)
    zx = lax.axis_index("trade") // NY
    pull = lax.dynamic_index_in_dim(mean_pullback.reshape(NZ * NX, 1, COLS, 1, LANES), zx, 0, False)
    state = shocks[:, :, 0]
    states = [state]
    for date in range(1, dates):
        state = pull * state + shocks[:, :, date]
        states.append(state)
    levels = jnp.stack(states, 2).astype(BF16).reshape(CHUNKS, COLS, ROWS, LANES)
    nets = values_and_nets(
        levels, sensitivity_tensor, moneyness_shift, signed_principal,
        deal_agreement_group, active_position_number,
    )
    nets = nets.reshape(CHUNKS, SETS_DEV, NY, dates, span)
    exposure = nets.transpose(3, 2, 0, 4, 1).reshape(dates, scen, SETS_DEV)
    mean = lax.psum(jnp.sum(exposure, axis=1), "scen") / (scen * lax.axis_size("scen"))
    return exposure, mean


def solution(mesh):
    in_specs = (
        P(None, "scen", "trade"), P("trade", None), P(), P(None, "trade"),
        P("trade"), P("trade"), P("trade"), P("trade"),
    )
    out_specs = (P(None, "scen", "trade"), P(None, "trade"))
    return jax.shard_map(
        on_device, mesh=mesh, in_specs=in_specs, out_specs=out_specs, check_vma=False
    )
```

```python
import functools
import jax
import jax.numpy as jnp
from jax import lax
from jax.experimental import pallas as pl
from jax.experimental.pallas import tpu as pltpu
from jax.sharding import PartitionSpec as P

F32, BF16 = jnp.float32, jnp.bfloat16
SETS_DEV = 16
NZ, NX, NY = 2, 4, 4
N_TRADE = NZ * NX * NY
CHUNKS = 4
COLS = 4
ROWS = 64
LANES = 128
TILE = 256
PARTS = (
    ((0, 3), (0, 32), ("z", "y", "x")),
    ((0, 3), (32, 32), ("z", "x", "y")),
    ((3, 1), (0, 64), ("x", "y", "z")),
)
STEPS = 5
DRAW_ORDERS = (("z", "x"), ("x", "z"))
DRAW_STEPS = 3
SLOTS = 10


def trade_place():
    me = lax.axis_index("trade")
    return {"z": me // (NX * NY), "x": (me // NY) % NX, "y": me % NY}


def trade_index(place):
    return (place["z"] * NX + place["x"]) * NY + place["y"]


def moved(place, axis, by):
    size = {"z": NZ, "x": NX, "y": NY}[axis]
    return dict(place, **{axis: (place[axis] + by) % size})


def part_steps(place, order):
    have = dict(place)
    steps = []
    for axis in order:
        if axis == "z":
            steps.append(
                (
                    [(dict(have), None, moved(place, "z", 1))],
                    [(dict(have, z=1 - place["z"]), None)],
                )
            )
        else:
            right, left = moved(place, axis, 1), moved(place, axis, 3)
            far = moved(place, axis, 2)
            at = lambda where: dict(have, **{axis: where[axis]})
            steps.append(
                (
                    [(at(place), None, right), (at(place), None, left)],
                    [(at(left), None), (at(right), None)],
                )
            )
            steps.append(
                (
                    [(at(left), 0, right), (at(right), 1, left)],
                    [(at(far), 0), (at(far), 1)],
                )
            )
        have[axis] = None
    return steps


def softplus(a):
    return jnp.maximum(a, 0.0) + jnp.log1p(jnp.exp(-jnp.abs(a)))


def factor_block(col, owner):
    return 8 * col + (owner if col % 2 == 0 else 7 - owner)


def column_home(col):
    return {3: (0, 0), 0: (0, 8), 2: (1, 0), 1: (1, 6)}[col]


def exposure_kernel(
    draws_hbm, root_hbm, sens_hbm, pull_ref, shift_ref, principal_ref, group_ref, live_ref,
    out_ref, mean_ref,
    draws, root, book, sens, member, weight, net, net_out, net_in, mean_in,
    draw_send, draw_recv, draw_ring_send, draw_ring_recv,
    root_send, root_recv, root_ring_send, root_ring_recv, twin_send, twin_recv,
    send_sems, recv_sems, own_sems, sens_sem, net_send_sem, net_recv_sems,
    mean_send, mean_recv,
):
    place = trade_place()
    me = trade_index(place)
    zx = place["z"] * NX + place["x"]
    scen = lax.axis_index("scen")
    scens = lax.axis_size("scen")
    core = scen % 2
    twin = scen + 1 - 2 * core
    positions = sens.shape[1]
    sets = member.shape[0]
    span = draws_hbm.shape[1] // NY

    def remote(src, dst, send, recv, **target):
        return pltpu.make_async_remote_copy(
            src_ref=src, dst_ref=dst, send_sem=send, recv_sem=recv,
            device_id=target, device_id_type=pl.DeviceIdType.MESH,
        )

    barrier = pltpu.get_barrier_semaphore()

    @pl.loop(1, N_TRADE)
    def _(step):
        pl.semaphore_signal(
            barrier, inc=1, device_id={"trade": (me + step) % N_TRADE},
            device_id_type=pl.DeviceIdType.MESH,
        )

    @pl.loop(1, scens)
    def _(step):
        pl.semaphore_signal(
            barrier, inc=1, device_id={"scen": (scen + step) % scens},
            device_id_type=pl.DeviceIdType.MESH,
        )

    pl.semaphore_wait(barrier, N_TRADE - 1 + scens - 1)

    def draw_rows(y):
        return draws_hbm.at[:, pl.ds(y * span, span), :]

    def draw_copy(by, source):
        return remote(
            draw_rows((place["y"] + by) % NY), draws.at[place["z"], place["x"], source],
            draw_send.at[by - 1], draw_recv.at[by - 1],
            trade=trade_index(moved(place, "y", by)),
        )

    own_draws = pltpu.make_async_copy(
        draw_rows(place["y"]), draws.at[place["z"], place["x"], place["y"]], own_sems.at[0]
    )
    own_draws.start()
    for by in range(1, NY):
        draw_copy(by, place["y"]).start()

    high_count, low_count = 8 - 2 * core, 2 + 2 * core
    kinds = ((3 - core, high_count, 0), (core, low_count, high_count))

    def root_block(kind, owner):
        col = kinds[kind][0]
        block = 8 * col + jnp.where(col % 2 == 0, owner, 7 - owner)
        return root_hbm.at[:, pl.ds(pl.multiple_of(block * LANES, LANES), LANES)]

    def root_slot(kind, source):
        return root.at[core, kinds[kind][2] + source, place["y"]]

    def root_copy(kind, owner, source):
        return remote(
            root_block(kind, owner), root_slot(kind, source),
            root_send.at[kind, owner], root_recv.at[kind, source],
            trade=owner * NY + place["y"],
        )

    def own_root(kind):
        return pltpu.make_async_copy(root_block(kind, zx), root_slot(kind, zx), own_sems.at[1 + kind])

    for kind in range(2):
        @pl.when(zx < kinds[kind][1])
        def _(kind=kind):
            own_root(kind).start()

            @pl.loop(1, NZ * NX)
            def _(step):
                root_copy(kind, (zx + step) % (NZ * NX), zx).start()

    fetch = pltpu.make_async_copy(sens_hbm, sens, sens_sem)
    fetch.start()

    draw_plans = [part_steps(place, order) for order in DRAW_ORDERS]

    def draw_ring(step, kind):
        for date, plan in enumerate(draw_plans):
            sends, recvs = plan[step]
            for way in range(len(sends)):
                coords, half = (sends if kind == "send" else recvs)[way][:2]
                target = sends[way][2]
                row, rows = 0, span
                if half is not None:
                    rows = span // 2
                    row = half * rows
                pick = [slice(None) if coords[a] is None else coords[a] for a in "zx"]
                ref = draws.at[pick[0], pick[1], :, date, pl.ds(row, rows), :]
                yield remote(
                    ref, ref, draw_ring_send.at[date, step, way], draw_ring_recv.at[date, step, way],
                    trade=trade_index(target),
                )

    def root_ring(step, kind):
        y = place["y"]
        right, left = moved(place, "y", 1), moved(place, "y", 3)
        far = (y + 2) % NY
        half = SLOTS // 2
        if step == 0:
            at = {"send": (y, y), "recv": (left["y"], right["y"])}[kind]
            refs = [root.at[core, :, a] for a in at]
        else:
            at = {"send": (left["y"], right["y"]), "recv": (far, far)}[kind]
            refs = [root.at[core, pl.ds(half * way, half), a] for way, a in enumerate(at)]
        for way, target in enumerate((right, left)):
            yield remote(
                refs[way], refs[way], root_ring_send.at[step, way], root_ring_recv.at[step, way],
                trade=trade_index(target),
            )

    def twin_copy(by, from_core):
        ref = root.at[from_core, :, (place["y"] + by) % NY]
        return remote(ref, ref, twin_send.at[by], twin_recv.at[by], scen=twin)

    weight[...] = jnp.where(
        lax.broadcasted_iota(jnp.int32, (1, positions), 1) < live_ref[...],
        principal_ref[...], 0.0,
    )

    own_draws.wait()
    for by in range(1, NY):
        draw_copy(by, (place["y"] + NY - by) % NY).wait_recv()
    for copy in draw_ring(0, "send"):
        copy.start()

    for kind in range(2):
        @pl.when(zx < kinds[kind][1])
        def _(kind=kind):
            own_root(kind).wait()

        @pl.loop(0, NZ * NX)
        def _(source, kind=kind):
            @pl.when(jnp.logical_and(source < kinds[kind][1], source != zx))
            def _():
                root_copy(kind, zx, source).wait_recv()
    for copy in root_ring(0, "send"):
        copy.start()
    twin_copy(0, core).start()

    for copy in draw_ring(0, "recv"):
        copy.wait_recv()
    for copy in draw_ring(1, "send"):
        copy.start()

    for copy in root_ring(0, "recv"):
        copy.wait_recv()
    for copy in root_ring(1, "send"):
        copy.start()
    twin_copy(1, core).start()
    twin_copy(3, core).start()

    for copy in draw_ring(1, "recv"):
        copy.wait_recv()
    for copy in draw_ring(2, "send"):
        copy.start()

    @pl.loop(0, positions // TILE)
    def _(tile):
        at = pl.ds(pl.multiple_of(tile * TILE, TILE), TILE)
        labels = lax.broadcasted_iota(jnp.int32, (sets, TILE), 0)
        member[:, at] = (labels == group_ref[:, at]).astype(F32).astype(BF16)

    for copy in root_ring(1, "recv"):
        copy.wait_recv()
    twin_copy(2, core).start()
    for by in range(NY):
        twin_copy(by, 1 - core).wait_recv()
    for copy in draw_ring(2, "recv"):
        copy.wait_recv()

    dates = draws.shape[3]
    part_rows = span // CHUNKS
    for col in range(COLS):
        home, slot = column_home(col)
        sources = [(s, y) for s in range(2 * (col + 1)) for y in range(NY)]
        left = jnp.concatenate(
            [draws[s // NX, s % NX, y].reshape(dates * span, LANES) for s, y in sources], axis=1
        )
        right = jnp.concatenate([root[home, slot + s, y] for s, y in sources], axis=0)
        shocks = jnp.dot(left, right, preferred_element_type=F32)
        pull = pull_ref[pl.ds(factor_block(col, zx), 1), :]
        state = jnp.zeros((span, LANES), F32)
        for date in range(dates):
            state = pull * state + shocks[date * span:(date + 1) * span]
            levels = state.astype(BF16)
            for chunk in range(CHUNKS):
                book[
                    chunk, place["z"], place["x"], col, place["y"],
                    pl.ds(date * part_rows, part_rows), :,
                ] = levels[chunk * part_rows:(chunk + 1) * part_rows]

    plans = [part_steps(place, order) for _, _, order in PARTS]

    def view(part, chunk, coords, half):
        (col, cols), (row, rows), _ = PARTS[part]
        if half is not None:
            rows = rows // 2
            row = row + half * rows
        pick = [slice(None) if coords[a] is None else coords[a] for a in "zxy"]
        return book.at[chunk, pick[0], pick[1], pl.ds(col, cols), pick[2], pl.ds(row, rows), :]

    def descriptors(part, step, chunk, kind):
        sends, recvs = plans[part][step]
        for way in range(len(sends)):
            if kind == "send":
                coords, half, target = sends[way]
            else:
                coords, half = recvs[way]
                target = place
            ref = view(part, chunk, coords, half)
            yield remote(
                ref, ref, send_sems.at[chunk, part, step, way], recv_sems.at[chunk, part, step, way],
                trade=trade_index(target),
            )

    def start(step, chunk):
        for part in range(len(PARTS)):
            for copy in descriptors(part, step, chunk, "send"):
                copy.start()

    def arrived(step, chunk):
        for part in range(len(PARTS)):
            for copy in descriptors(part, step, chunk, "recv"):
                copy.wait_recv()

    @pl.loop(0, CHUNKS)
    def _(chunk):
        start(0, chunk)

    for step in (1, 2):
        @pl.loop(0, CHUNKS)
        def _(chunk, step=step):
            arrived(step - 1, chunk)
            start(step, chunk)

    fetch.wait()

    def net_copy(chunk, target):
        return remote(
            net_out.at[chunk, target], net_in.at[chunk, me],
            net_send_sem, net_recv_sems.at[chunk], trade=target,
        )

    def compute(chunk):
        net[...] = jnp.zeros_like(net)
        levels = jnp.concatenate(
            [
                book[chunk, owner // NX, owner % NX, col].reshape(NY * ROWS, LANES)
                for col in range(COLS) for owner in range(NZ * NX)[:: 1 - 2 * (col % 2)]
            ],
            axis=1,
        )

        @pl.loop(0, positions // TILE)
        def _(tile):
            at = pl.ds(pl.multiple_of(tile * TILE, TILE), TILE)
            moneyness = jnp.dot(levels, sens[:, at], preferred_element_type=F32)
            values = weight[:, at] * softplus(moneyness + shift_ref[:, at])
            net[...] += lax.dot_general(
                member[:, at], values.astype(BF16), (((1,), (1,)), ((), ())),
                preferred_element_type=F32,
            )

        net_out[chunk] = net[...].astype(BF16).reshape(N_TRADE, SETS_DEV, NY * ROWS)

        @pl.loop(1, N_TRADE)
        def _(step):
            net_copy(chunk, (me + step) % N_TRADE).start()

        net_in[chunk, me] = net_out[chunk, me]

    @pl.loop(0, CHUNKS + 2)
    def _(tick):
        @pl.when(tick < CHUNKS)
        def _():
            arrived(2, tick)
            start(3, tick)

        @pl.when(jnp.logical_and(tick >= 1, tick < CHUNKS + 1))
        def _():
            arrived(3, tick - 1)
            start(4, tick - 1)

        @pl.when(tick >= 2)
        def _():
            arrived(4, tick - 2)
            compute(tick - 2)

    @pl.loop(0, CHUNKS)
    def _(chunk):
        for part in range(len(PARTS)):
            for step in range(STEPS):
                for copy in descriptors(part, step, chunk, "send"):
                    copy.wait_send()

        whole = remote(
            net_out.at[chunk, pl.ds(0, N_TRADE - 1)], net_in.at[chunk, pl.ds(0, N_TRADE - 1)],
            net_send_sem, net_recv_sems.at[chunk], trade=me,
        )
        whole.wait_send()
        whole.wait_recv()
        total = jnp.zeros((SETS_DEV, NY * ROWS), F32)
        for sender in range(N_TRADE):
            total = total + net_in[chunk, sender].astype(F32)
        net[pl.ds(pl.multiple_of(chunk * SETS_DEV, SETS_DEV), SETS_DEV), :] = jnp.maximum(total, 0.0)

    lane = lax.broadcasted_iota(jnp.int32, (SETS_DEV, LANES), 1)
    sums = jnp.zeros((SETS_DEV, LANES), F32)
    for date in range(dates):
        strip = jnp.concatenate(
            [
                net[chunk * SETS_DEV:(chunk + 1) * SETS_DEV, y * ROWS + date * part_rows:][:, :part_rows]
                for y in range(NY) for chunk in range(CHUNKS)
            ],
            axis=1,
        )
        out_ref[date] = strip
        sums = jnp.where(lane == date, jnp.sum(strip, axis=1, keepdims=True), sums)
    mean_in[scen] = sums

    def mean_copy(by, slot):
        return remote(
            mean_in.at[slot], mean_in.at[slot], mean_send.at[by - 1], mean_recv.at[by - 1],
            scen=(scen + by) % scens,
        )

    for by in range(1, scens):
        mean_copy(by, scen).start()

    for by in range(1, NY):
        draw_copy(by, place["y"]).wait_send()
    for step in range(DRAW_STEPS):
        for copy in draw_ring(step, "send"):
            copy.wait_send()
    for kind in range(2):
        @pl.when(zx < kinds[kind][1])
        def _(kind=kind):
            @pl.loop(1, NZ * NX)
            def _(step):
                root_copy(kind, (zx + step) % (NZ * NX), zx).wait_send()
    for step in range(2):
        for copy in root_ring(step, "send"):
            copy.wait_send()
    for by in range(NY):
        twin_copy(by, core).wait_send()

    for by in range(1, scens):
        mean_copy(by, (scen + scens - by) % scens).wait_recv()
        mean_copy(by, scen).wait_send()
    mean_ref[...] = jnp.sum(mean_in[...], axis=0) / (scens * NY * span)


def exposures(draws, root, sensitivity, pull, shift, principal, group, live):
    dates, scen, _ = draws.shape
    positions = sensitivity.shape[1]
    sets = SETS_DEV * N_TRADE
    span = scen // NY
    vmem = pl.BlockSpec(memory_space=pltpu.VMEM)
    hbm = pl.BlockSpec(memory_space=pl.ANY)
    dma = pltpu.SemaphoreType.DMA
    return pl.pallas_call(
        exposure_kernel,
        out_shape=(
            jax.ShapeDtypeStruct((dates, SETS_DEV, scen), F32),
            jax.ShapeDtypeStruct((SETS_DEV, LANES), F32),
        ),
        in_specs=[hbm, hbm, hbm, vmem, vmem, vmem, vmem, vmem],
        out_specs=(vmem, vmem),
        scratch_shapes=[
            pltpu.VMEM((NZ, NX, NY, dates, span, LANES), BF16),
            pltpu.VMEM((2, SLOTS, NY, LANES, LANES), BF16),
            pltpu.VMEM((CHUNKS, NZ, NX, COLS, NY, ROWS, LANES), BF16),
            pltpu.VMEM(sensitivity.shape, BF16),
            pltpu.VMEM((sets, positions), BF16),
            pltpu.VMEM((1, positions), F32),
            pltpu.VMEM((sets, NY * ROWS), F32),
            pltpu.VMEM((CHUNKS, N_TRADE, SETS_DEV, NY * ROWS), BF16),
            pltpu.VMEM((CHUNKS, N_TRADE, SETS_DEV, NY * ROWS), BF16),
            pltpu.VMEM((lax.axis_size("scen"), SETS_DEV, LANES), F32),
            dma((NY - 1,)), dma((NY - 1,)),
            dma((dates, DRAW_STEPS, 2)), dma((dates, DRAW_STEPS, 2)),
            dma((2, NZ * NX)), dma((2, NZ * NX)),
            dma((2, 2)), dma((2, 2)), dma((NY,)), dma((NY,)),
            dma((CHUNKS, len(PARTS), STEPS, 2)), dma((CHUNKS, len(PARTS), STEPS, 2)),
            dma((3,)), dma, dma, dma((CHUNKS,)),
            dma((lax.axis_size("scen") - 1,)), dma((lax.axis_size("scen") - 1,)),
        ],
        compiler_params=pltpu.CompilerParams(
            collective_id=1, has_side_effects=True, vmem_limit_bytes=58 * 2**20
        ),
        cost_estimate=pl.CostEstimate(
            flops=2 * 1024 * positions * (4096 + sets), bytes_accessed=17 << 20, transcendentals=0
        ),
        name="exposures",
    )(
        draws, root, sensitivity, pull.reshape(-1, LANES), shift.reshape(1, -1),
        principal.reshape(1, -1), group.reshape(1, -1), live.reshape(1, 1),
    )


def on_device(
    normal_draws, covariance_root, mean_pullback, sensitivity_tensor,
    moneyness_shift, signed_principal, deal_agreement_group, active_position_number,
):
    exposure, mean = exposures(
        normal_draws, covariance_root, sensitivity_tensor, mean_pullback, moneyness_shift,
        signed_principal, deal_agreement_group, active_position_number,
    )
    return exposure.transpose(0, 2, 1), mean[:, : normal_draws.shape[0]].T


def solution(mesh):
    in_specs = (
        P(None, "scen", "trade"), P("trade", None), P(), P(None, "trade"),
        P("trade"), P("trade"), P("trade"), P("trade"),
    )
    out_specs = (P(None, "scen", "trade"), P(None, "trade"))
    return jax.shard_map(
        on_device, mesh=mesh, in_specs=in_specs, out_specs=out_specs, check_vma=False
    )
```

```python
import functools
import jax
import jax.numpy as jnp
from jax import lax
from jax.experimental import pallas as pl
from jax.experimental.pallas import tpu as pltpu
from jax.sharding import PartitionSpec as P

F32, BF16 = jnp.float32, jnp.bfloat16
SETS_DEV = 16
NZ, NX, NY = 2, 4, 4
N_TRADE = NZ * NX * NY
CHUNKS = 4
COLS = 4
ROWS = 64
LANES = 128
TILE = 512
HALVES = 2
PARTS = (
    ((0, 3), (0, 32), ("z", "y", "x")),
    ((0, 3), (32, 32), ("z", "x", "y")),
    ((3, 1), (0, 64), ("x", "y", "z")),
)
STEPS = 5
DRAW_ORDERS = (("z", "x"), ("x", "z"))
DRAW_STEPS = 3
SLOTS = 10


def trade_place():
    me = lax.axis_index("trade")
    return {"z": me // (NX * NY), "x": (me // NY) % NX, "y": me % NY}


def trade_index(place):
    return (place["z"] * NX + place["x"]) * NY + place["y"]


def moved(place, axis, by):
    size = {"z": NZ, "x": NX, "y": NY}[axis]
    return dict(place, **{axis: (place[axis] + by) % size})


def part_steps(place, order):
    have = dict(place)
    steps = []
    for axis in order:
        if axis == "z":
            steps.append(
                (
                    [(dict(have), None, moved(place, "z", 1))],
                    [(dict(have, z=1 - place["z"]), None)],
                )
            )
        else:
            right, left = moved(place, axis, 1), moved(place, axis, 3)
            far = moved(place, axis, 2)
            at = lambda where: dict(have, **{axis: where[axis]})
            steps.append(
                (
                    [(at(place), None, right), (at(place), None, left)],
                    [(at(left), None), (at(right), None)],
                )
            )
            steps.append(
                (
                    [(at(left), 0, right), (at(right), 1, left)],
                    [(at(far), 0), (at(far), 1)],
                )
            )
        have[axis] = None
    return steps


def softplus(a):
    return jnp.maximum(a, 0.0) + jnp.log(1.0 + jnp.exp(-jnp.abs(a)))


def factor_block(col, owner):
    return 8 * col + (owner if col % 2 == 0 else 7 - owner)


def column_home(col):
    return {3: (0, 0), 0: (0, 8), 2: (1, 0), 1: (1, 6)}[col]


def exposure_kernel(
    draws_hbm, root_hbm, sens_hbm, pull_ref, shift_ref, principal_ref, group_ref, live_ref,
    out_ref, mean_ref,
    draws, root, book, sens, member, weight, net, prices, net_out, net_in, mean_in,
    draw_send, draw_recv, draw_ring_send, draw_ring_recv,
    root_send, root_recv, root_ring_send, root_ring_recv, twin_send, twin_recv,
    send_sems, recv_sems, own_sems, sens_sem, net_send_sem, net_recv_sems,
    mean_send, mean_recv,
):
    place = trade_place()
    me = trade_index(place)
    zx = place["z"] * NX + place["x"]
    scen = lax.axis_index("scen")
    scens = lax.axis_size("scen")
    core = scen % 2
    twin = scen + 1 - 2 * core
    positions = sens.shape[1]
    sets = member.shape[0]
    span = draws_hbm.shape[1] // NY

    def remote(src, dst, send, recv, **target):
        return pltpu.make_async_remote_copy(
            src_ref=src, dst_ref=dst, send_sem=send, recv_sem=recv,
            device_id=target, device_id_type=pl.DeviceIdType.MESH,
        )

    barrier = pltpu.get_barrier_semaphore()

    @pl.loop(1, N_TRADE)
    def _(step):
        pl.semaphore_signal(
            barrier, inc=1, device_id={"trade": (me + step) % N_TRADE},
            device_id_type=pl.DeviceIdType.MESH,
        )

    @pl.loop(1, scens)
    def _(step):
        pl.semaphore_signal(
            barrier, inc=1, device_id={"scen": (scen + step) % scens},
            device_id_type=pl.DeviceIdType.MESH,
        )

    pl.semaphore_wait(barrier, N_TRADE - 1 + scens - 1)

    def draw_rows(y):
        return draws_hbm.at[:, pl.ds(y * span, span), :]

    def draw_copy(by, source):
        return remote(
            draw_rows((place["y"] + by) % NY), draws.at[place["z"], place["x"], source],
            draw_send.at[by - 1], draw_recv.at[by - 1],
            trade=trade_index(moved(place, "y", by)),
        )

    own_draws = pltpu.make_async_copy(
        draw_rows(place["y"]), draws.at[place["z"], place["x"], place["y"]], own_sems.at[0]
    )
    own_draws.start()
    for by in range(1, NY):
        draw_copy(by, place["y"]).start()

    high_count, low_count = 8 - 2 * core, 2 + 2 * core
    kinds = ((3 - core, high_count, 0), (core, low_count, high_count))

    def root_block(kind, owner):
        col = kinds[kind][0]
        block = 8 * col + jnp.where(col % 2 == 0, owner, 7 - owner)
        return root_hbm.at[:, pl.ds(pl.multiple_of(block * LANES, LANES), LANES)]

    def root_slot(kind, source):
        return root.at[core, kinds[kind][2] + source, place["y"]]

    def root_copy(kind, owner, source):
        return remote(
            root_block(kind, owner), root_slot(kind, source),
            root_send.at[kind, owner], root_recv.at[kind, source],
            trade=owner * NY + place["y"],
        )

    def own_root(kind):
        return pltpu.make_async_copy(root_block(kind, zx), root_slot(kind, zx), own_sems.at[1 + kind])

    for kind in range(2):
        @pl.when(zx < kinds[kind][1])
        def _(kind=kind):
            own_root(kind).start()

            @pl.loop(1, NZ * NX)
            def _(step):
                root_copy(kind, (zx + step) % (NZ * NX), zx).start()

    fetch = pltpu.make_async_copy(sens_hbm, sens, sens_sem)
    fetch.start()

    draw_plans = [part_steps(place, order) for order in DRAW_ORDERS]

    def draw_ring(step, kind, part):
        for date, plan in enumerate(draw_plans):
            sends, recvs = plan[step]
            for way in range(len(sends)):
                coords, half = (sends if kind == "send" else recvs)[way][:2]
                target = sends[way][2]
                rows = span // HALVES
                row = part * rows
                if half is not None:
                    rows = rows // 2
                    row = row + half * rows
                pick = [slice(None) if coords[a] is None else coords[a] for a in "zx"]
                ref = draws.at[pick[0], pick[1], :, date, pl.ds(row, rows), :]
                yield remote(
                    ref, ref, draw_ring_send.at[part, date, step, way],
                    draw_ring_recv.at[part, date, step, way],
                    trade=trade_index(target),
                )

    def root_ring(step, kind):
        y = place["y"]
        right, left = moved(place, "y", 1), moved(place, "y", 3)
        far = (y + 2) % NY
        half = SLOTS // 2
        if step == 0:
            at = {"send": (y, y), "recv": (left["y"], right["y"])}[kind]
            refs = [root.at[core, :, a] for a in at]
        else:
            at = {"send": (left["y"], right["y"]), "recv": (far, far)}[kind]
            refs = [root.at[core, pl.ds(half * way, half), a] for way, a in enumerate(at)]
        for way, target in enumerate((right, left)):
            yield remote(
                refs[way], refs[way], root_ring_send.at[step, way], root_ring_recv.at[step, way],
                trade=trade_index(target),
            )

    def twin_copy(by, from_core):
        ref = root.at[from_core, :, (place["y"] + by) % NY]
        return remote(ref, ref, twin_send.at[by], twin_recv.at[by], scen=twin)

    weight[...] = jnp.where(
        lax.broadcasted_iota(jnp.int32, (1, positions), 1) < live_ref[...],
        principal_ref[...], 0.0,
    )

    own_draws.wait()
    for by in range(1, NY):
        draw_copy(by, (place["y"] + NY - by) % NY).wait_recv()
    def draw_start(step, part):
        for copy in draw_ring(step, "send", part):
            copy.start()

    def draw_arrived(step, part):
        for copy in draw_ring(step, "recv", part):
            copy.wait_recv()

    for part in range(HALVES):
        draw_start(0, part)

    for kind in range(2):
        @pl.when(zx < kinds[kind][1])
        def _(kind=kind):
            own_root(kind).wait()

        @pl.loop(0, NZ * NX)
        def _(source, kind=kind):
            @pl.when(jnp.logical_and(source < kinds[kind][1], source != zx))
            def _():
                root_copy(kind, zx, source).wait_recv()
    for copy in root_ring(0, "send"):
        copy.start()
    twin_copy(0, core).start()

    for part in range(HALVES):
        draw_arrived(0, part)
        draw_start(1, part)

    for copy in root_ring(0, "recv"):
        copy.wait_recv()
    for copy in root_ring(1, "send"):
        copy.start()
    twin_copy(1, core).start()
    twin_copy(3, core).start()

    for part in range(HALVES):
        draw_arrived(1, part)
        draw_start(2, part)

    for copy in root_ring(1, "recv"):
        copy.wait_recv()
    twin_copy(2, core).start()

    @pl.loop(0, positions // TILE)
    def _(tile):
        at = pl.ds(pl.multiple_of(tile * TILE, TILE), TILE)
        labels = lax.broadcasted_iota(jnp.int32, (sets, TILE), 0)
        member[:, at] = (labels == group_ref[:, at]).astype(F32).astype(BF16)

    for by in range(NY):
        twin_copy(by, 1 - core).wait_recv()

    dates = draws.shape[3]
    part_rows = span // CHUNKS

    def make_levels(part):
        rows = span // HALVES
        for col in range(COLS):
            home, slot = column_home(col)
            sources = [(s, y) for s in range(2 * (col + 1)) for y in range(NY)]
            left = jnp.concatenate(
                [
                    draws[s // NX, s % NX, y, :, pl.ds(part * rows, rows), :].reshape(dates * rows, LANES)
                    for s, y in sources
                ],
                axis=1,
            )
            right = jnp.concatenate([root[home, slot + s, y] for s, y in sources], axis=0)
            shocks = jnp.dot(left, right, preferred_element_type=F32)
            pull = pull_ref[pl.ds(factor_block(col, zx), 1), :]
            state = jnp.zeros((rows, LANES), F32)
            for date in range(dates):
                state = pull * state + shocks[date * rows:(date + 1) * rows]
                levels = state.astype(BF16)
                for chunk in range(CHUNKS // HALVES):
                    book[
                        part * (CHUNKS // HALVES) + chunk, place["z"], place["x"], col, place["y"],
                        pl.ds(date * part_rows, part_rows), :,
                    ] = levels[chunk * part_rows:(chunk + 1) * part_rows]

    plans = [part_steps(place, order) for _, _, order in PARTS]

    def view(part, chunk, coords, half):
        (col, cols), (row, rows), _ = PARTS[part]
        if half is not None:
            rows = rows // 2
            row = row + half * rows
        pick = [slice(None) if coords[a] is None else coords[a] for a in "zxy"]
        return book.at[chunk, pick[0], pick[1], pl.ds(col, cols), pick[2], pl.ds(row, rows), :]

    def descriptors(part, step, chunk, kind):
        sends, recvs = plans[part][step]
        for way in range(len(sends)):
            if kind == "send":
                coords, half, target = sends[way]
            else:
                coords, half = recvs[way]
                target = place
            ref = view(part, chunk, coords, half)
            yield remote(
                ref, ref, send_sems.at[chunk, part, step, way], recv_sems.at[chunk, part, step, way],
                trade=trade_index(target),
            )

    def start(step, chunk):
        for part in range(len(PARTS)):
            for copy in descriptors(part, step, chunk, "send"):
                copy.start()

    def arrived(step, chunk):
        for part in range(len(PARTS)):
            for copy in descriptors(part, step, chunk, "recv"):
                copy.wait_recv()

    for part in range(HALVES):
        draw_arrived(2, part)
        make_levels(part)
        for chunk in range(CHUNKS // HALVES):
            start(0, part * (CHUNKS // HALVES) + chunk)


    def net_copy(chunk, target):
        return remote(
            net_out.at[chunk, target], net_in.at[chunk, me],
            net_send_sem, net_recv_sems.at[chunk], trade=target,
        )

    def compute(chunk):
        net[...] = jnp.zeros_like(net)
        levels = jnp.concatenate(
            [
                book[chunk, owner // NX, owner % NX, col].reshape(NY * ROWS, LANES)
                for col in range(COLS) for owner in range(NZ * NX)[:: 1 - 2 * (col % 2)]
            ],
            axis=1,
        )

        def strip(tile):
            return pl.ds(pl.multiple_of(tile * TILE, TILE), TILE)

        def price(tile, slot):
            prices[slot] = jnp.dot(levels, sens[:, strip(tile)], preferred_element_type=F32)

        def settle(tile, slot):
            at = strip(tile)
            values = weight[:, at] * softplus(prices[slot] + shift_ref[:, at])
            net[...] += lax.dot_general(
                member[:, at], values.astype(BF16), (((1,), (1,)), ((), ())),
                preferred_element_type=F32,
            )

        tiles = positions // TILE
        price(0, 0)

        @pl.loop(0, tiles // 2 - 1)
        def _(pair):
            price(2 * pair + 1, 1)
            settle(2 * pair, 0)
            price(2 * pair + 2, 0)
            settle(2 * pair + 1, 1)

        price(tiles - 1, 1)
        settle(tiles - 2, 0)
        settle(tiles - 1, 1)

        net_out[chunk] = net[...].astype(BF16).reshape(N_TRADE, SETS_DEV, NY * ROWS)

        @pl.loop(1, N_TRADE)
        def _(step):
            net_copy(chunk, (me + step) % N_TRADE).start()

        net_in[chunk, me] = net_out[chunk, me]

    @pl.loop(0, CHUNKS + STEPS - 1)
    def _(tick):
        for step in reversed(range(1, STEPS)):
            chunk = tick - (step - 1)

            @pl.when(jnp.logical_and(chunk >= 0, chunk < CHUNKS))
            def _(step=step, chunk=chunk):
                arrived(step - 1, chunk)
                start(step, chunk)

        last = tick - (STEPS - 1)

        @pl.when(last == 0)
        def _():
            fetch.wait()

        @pl.when(last >= 0)
        def _():
            arrived(STEPS - 1, last)
            compute(last)

    for by in range(1, NY):
        draw_copy(by, place["y"]).wait_send()
    for part in range(HALVES):
        for step in range(DRAW_STEPS):
            for copy in draw_ring(step, "send", part):
                copy.wait_send()
    for kind in range(2):
        @pl.when(zx < kinds[kind][1])
        def _(kind=kind):
            @pl.loop(1, NZ * NX)
            def _(step):
                root_copy(kind, (zx + step) % (NZ * NX), zx).wait_send()
    for step in range(2):
        for copy in root_ring(step, "send"):
            copy.wait_send()
    for by in range(NY):
        twin_copy(by, core).wait_send()

    @pl.loop(0, CHUNKS)
    def _(chunk):
        for part in range(len(PARTS)):
            for step in range(STEPS):
                for copy in descriptors(part, step, chunk, "send"):
                    copy.wait_send()

    @pl.loop(0, CHUNKS)
    def _(chunk):
        whole = remote(
            net_out.at[chunk, pl.ds(0, N_TRADE - 1)], net_in.at[chunk, pl.ds(0, N_TRADE - 1)],
            net_send_sem, net_recv_sems.at[chunk], trade=me,
        )
        whole.wait_send()
        whole.wait_recv()
        total = jnp.zeros((SETS_DEV, NY * ROWS), F32)
        for sender in range(N_TRADE):
            total = total + net_in[chunk, sender].astype(F32)
        net[pl.ds(pl.multiple_of(chunk * SETS_DEV, SETS_DEV), SETS_DEV), :] = jnp.maximum(total, 0.0)

    mean_in[scen] = jnp.zeros(mean_in.shape[1:], F32)
    down = lax.broadcasted_iota(jnp.int32, (SETS_DEV, LANES), 0)
    across = lax.broadcasted_iota(jnp.int32, (SETS_DEV, LANES), 1)
    for date in range(dates):
        strip = jnp.concatenate(
            [
                net[chunk * SETS_DEV:(chunk + 1) * SETS_DEV, y * ROWS + date * part_rows:][:, :part_rows]
                for y in range(NY) for chunk in range(CHUNKS)
            ],
            axis=1,
        )
        out_ref[date] = strip
        sums = jnp.where(down == across, jnp.sum(strip, axis=1, keepdims=True), 0.0)
        mean_in[scen, pl.ds(date, 1), :] = jnp.sum(sums, axis=0, keepdims=True)

    def mean_copy(by, slot):
        return remote(
            mean_in.at[slot], mean_in.at[slot], mean_send.at[by - 1], mean_recv.at[by - 1],
            scen=(scen + by) % scens,
        )

    for by in range(1, scens):
        mean_copy(by, scen).start()

    for by in range(1, scens):
        mean_copy(by, (scen + scens - by) % scens).wait_recv()
        mean_copy(by, scen).wait_send()
    total = jnp.sum(mean_in[...], axis=0) / (scens * NY * span)
    mean_ref[...] = total[:dates, :SETS_DEV]


def exposures(draws, root, sensitivity, pull, shift, principal, group, live):
    dates, scen, _ = draws.shape
    positions = sensitivity.shape[1]
    sets = SETS_DEV * N_TRADE
    span = scen // NY
    vmem = pl.BlockSpec(memory_space=pltpu.VMEM)
    hbm = pl.BlockSpec(memory_space=pl.ANY)
    dma = pltpu.SemaphoreType.DMA
    return pl.pallas_call(
        exposure_kernel,
        out_shape=(
            jax.ShapeDtypeStruct((dates, SETS_DEV, scen), F32),
            jax.ShapeDtypeStruct((dates, SETS_DEV), F32),
        ),
        in_specs=[hbm, hbm, hbm, vmem, vmem, vmem, vmem, vmem],
        out_specs=(vmem, vmem),
        scratch_shapes=[
            pltpu.VMEM((NZ, NX, NY, dates, span, LANES), BF16),
            pltpu.VMEM((2, SLOTS, NY, LANES, LANES), BF16),
            pltpu.VMEM((CHUNKS, NZ, NX, COLS, NY, ROWS, LANES), BF16),
            pltpu.VMEM(sensitivity.shape, BF16),
            pltpu.VMEM((sets, positions), BF16),
            pltpu.VMEM((1, positions), F32),
            pltpu.VMEM((sets, NY * ROWS), F32),
            pltpu.VMEM((2, NY * ROWS, TILE), F32),
            pltpu.VMEM((CHUNKS, N_TRADE, SETS_DEV, NY * ROWS), BF16),
            pltpu.VMEM((CHUNKS, N_TRADE, SETS_DEV, NY * ROWS), BF16),
            pltpu.VMEM((lax.axis_size("scen"), 8, LANES), F32),
            dma((NY - 1,)), dma((NY - 1,)),
            dma((HALVES, dates, DRAW_STEPS, 2)), dma((HALVES, dates, DRAW_STEPS, 2)),
            dma((2, NZ * NX)), dma((2, NZ * NX)),
            dma((2, 2)), dma((2, 2)), dma((NY,)), dma((NY,)),
            dma((CHUNKS, len(PARTS), STEPS, 2)), dma((CHUNKS, len(PARTS), STEPS, 2)),
            dma((3,)), dma, dma, dma((CHUNKS,)),
            dma((lax.axis_size("scen") - 1,)), dma((lax.axis_size("scen") - 1,)),
        ],
        compiler_params=pltpu.CompilerParams(
            collective_id=1, has_side_effects=True, vmem_limit_bytes=58 * 2**20
        ),
        cost_estimate=pl.CostEstimate(
            flops=2 * 1024 * positions * (4096 + sets), bytes_accessed=17 << 20, transcendentals=0
        ),
        name="exposures",
    )(
        draws, root, sensitivity, pull.reshape(-1, LANES), shift.reshape(1, -1),
        principal.reshape(1, -1), group.reshape(1, -1), live.reshape(1, 1),
    )


def on_device(
    normal_draws, covariance_root, mean_pullback, sensitivity_tensor,
    moneyness_shift, signed_principal, deal_agreement_group, active_position_number,
):
    exposure, mean = exposures(
        normal_draws, covariance_root, sensitivity_tensor, mean_pullback, moneyness_shift,
        signed_principal, deal_agreement_group, active_position_number,
    )
    return exposure.transpose(0, 2, 1), mean


def solution(mesh):
    in_specs = (
        P(None, "scen", "trade"), P("trade", None), P(), P(None, "trade"),
        P("trade"), P("trade"), P("trade"), P("trade"),
    )
    out_specs = (P(None, "scen", "trade"), P(None, "trade"))
    return jax.shard_map(
        on_device, mesh=mesh, in_specs=in_specs, out_specs=out_specs, check_vma=False
    )
```

```python
import functools
import jax
import jax.numpy as jnp
from jax import lax
from jax.experimental import pallas as pl
from jax.experimental.pallas import tpu as pltpu
from jax.sharding import PartitionSpec as P

F32, BF16 = jnp.float32, jnp.bfloat16
SETS_DEV = 16
NZ, NX, NY = 2, 4, 4
N_TRADE = NZ * NX * NY
CHUNKS = 4
COLS = 4
ROWS = 64
LANES = 128
TILE = 512
HALVES = 2
PARTS = (
    ((0, 3), (0, 32), ("z", "y", "x")),
    ((0, 3), (32, 32), ("z", "x", "y")),
    ((3, 1), (0, 64), ("x", "y", "z")),
)
STEPS = 5
DRAW_ORDERS = (("z", "x"), ("x", "z"))
DRAW_STEPS = 3
SLOTS = 10


def trade_place():
    me = lax.axis_index("trade")
    return {"z": me // (NX * NY), "x": (me // NY) % NX, "y": me % NY}


def trade_index(place):
    return (place["z"] * NX + place["x"]) * NY + place["y"]


def moved(place, axis, by):
    size = {"z": NZ, "x": NX, "y": NY}[axis]
    return dict(place, **{axis: (place[axis] + by) % size})


def part_steps(place, order):
    have = dict(place)
    steps = []
    for axis in order:
        if axis == "z":
            steps.append(
                (
                    [(dict(have), None, moved(place, "z", 1))],
                    [(dict(have, z=1 - place["z"]), None)],
                )
            )
        else:
            right, left = moved(place, axis, 1), moved(place, axis, 3)
            far = moved(place, axis, 2)
            at = lambda where: dict(have, **{axis: where[axis]})
            steps.append(
                (
                    [(at(place), None, right), (at(place), None, left)],
                    [(at(left), None), (at(right), None)],
                )
            )
            steps.append(
                (
                    [(at(left), 0, right), (at(right), 1, left)],
                    [(at(far), 0), (at(far), 1)],
                )
            )
        have[axis] = None
    return steps


def hand_on(arrivals, sends, pairwise):
    arrivals, sends = list(arrivals), list(sends)
    if pairwise:
        for arrival, send in zip(arrivals, sends):
            arrival.wait_recv()
            send.start()
    else:
        for arrival in arrivals:
            arrival.wait_recv()
        for send in sends:
            send.start()


def softplus(a):
    return jnp.maximum(a, 0.0) + jnp.log(1.0 + jnp.exp(-jnp.abs(a)))


def factor_block(col, owner):
    return 8 * col + (owner if col % 2 == 0 else 7 - owner)


def column_home(col):
    return {3: (0, 0), 0: (0, 8), 2: (1, 0), 1: (1, 6)}[col]


def exposure_kernel(
    draws_hbm, root_hbm, sens_hbm, pull_ref, shift_ref, principal_ref, group_ref, live_ref,
    out_ref, mean_ref,
    draws, root, book, sens, member, weight, net, prices, net_out, net_in, mean_in,
    draw_send, draw_recv, draw_ring_send, draw_ring_recv,
    root_send, root_recv, root_ring_send, root_ring_recv, twin_send, twin_recv,
    send_sems, recv_sems, own_sems, sens_sem, net_send_sem, net_recv_sems,
    mean_send, mean_recv,
):
    place = trade_place()
    me = trade_index(place)
    zx = place["z"] * NX + place["x"]
    scen = lax.axis_index("scen")
    scens = lax.axis_size("scen")
    core = scen % 2
    twin = scen + 1 - 2 * core
    positions = sens.shape[1]
    sets = member.shape[0]
    span = draws_hbm.shape[1] // NY

    def remote(src, dst, send, recv, **target):
        return pltpu.make_async_remote_copy(
            src_ref=src, dst_ref=dst, send_sem=send, recv_sem=recv,
            device_id=target, device_id_type=pl.DeviceIdType.MESH,
        )

    barrier = pltpu.get_barrier_semaphore()

    @pl.loop(1, N_TRADE)
    def _(step):
        pl.semaphore_signal(
            barrier, inc=1, device_id={"trade": (me + step) % N_TRADE},
            device_id_type=pl.DeviceIdType.MESH,
        )

    @pl.loop(1, scens)
    def _(step):
        pl.semaphore_signal(
            barrier, inc=1, device_id={"scen": (scen + step) % scens},
            device_id_type=pl.DeviceIdType.MESH,
        )

    pl.semaphore_wait(barrier, N_TRADE - 1 + scens - 1)

    def draw_rows(y):
        return draws_hbm.at[:, pl.ds(y * span, span), :]

    def draw_copy(by, source):
        return remote(
            draw_rows((place["y"] + by) % NY), draws.at[place["z"], place["x"], source],
            draw_send.at[by - 1], draw_recv.at[by - 1],
            trade=trade_index(moved(place, "y", by)),
        )

    own_draws = pltpu.make_async_copy(
        draw_rows(place["y"]), draws.at[place["z"], place["x"], place["y"]], own_sems.at[0]
    )
    own_draws.start()
    for by in range(1, NY):
        draw_copy(by, place["y"]).start()

    high_count, low_count = 8 - 2 * core, 2 + 2 * core
    kinds = ((3 - core, high_count, 0), (core, low_count, high_count))

    def root_block(kind, owner):
        col = kinds[kind][0]
        block = 8 * col + jnp.where(col % 2 == 0, owner, 7 - owner)
        return root_hbm.at[:, pl.ds(pl.multiple_of(block * LANES, LANES), LANES)]

    def root_slot(kind, source):
        return root.at[core, kinds[kind][2] + source, place["y"]]

    def root_copy(kind, owner, source):
        return remote(
            root_block(kind, owner), root_slot(kind, source),
            root_send.at[kind, owner], root_recv.at[kind, source],
            trade=owner * NY + place["y"],
        )

    def own_root(kind):
        return pltpu.make_async_copy(root_block(kind, zx), root_slot(kind, zx), own_sems.at[1 + kind])

    for kind in range(2):
        @pl.when(zx < kinds[kind][1])
        def _(kind=kind):
            own_root(kind).start()

            @pl.loop(1, NZ * NX)
            def _(step):
                root_copy(kind, (zx + step) % (NZ * NX), zx).start()

    fetch = pltpu.make_async_copy(sens_hbm, sens, sens_sem)
    fetch.start()

    draw_plans = [part_steps(place, order) for order in DRAW_ORDERS]

    def draw_ring(step, kind, part, only=None):
        for date, plan in reversed(list(enumerate(draw_plans))):
            if only is not None and date != only:
                continue
            sends, recvs = plan[step]
            for way in range(len(sends)):
                coords, half = (sends if kind == "send" else recvs)[way][:2]
                target = sends[way][2]
                rows = span // HALVES
                row = part * rows
                if half is not None:
                    rows = rows // 2
                    row = row + half * rows
                pick = [slice(None) if coords[a] is None else coords[a] for a in "zx"]
                ref = draws.at[pick[0], pick[1], :, date, pl.ds(row, rows), :]
                yield remote(
                    ref, ref, draw_ring_send.at[part, date, step, way],
                    draw_ring_recv.at[part, date, step, way],
                    trade=trade_index(target),
                )

    def root_ring(step, kind):
        y = place["y"]
        right, left = moved(place, "y", 1), moved(place, "y", 3)
        far = (y + 2) % NY
        half = SLOTS // 2
        if step == 0:
            at = {"send": (y, y), "recv": (left["y"], right["y"])}[kind]
            refs = [root.at[core, :, a] for a in at]
        else:
            at = {"send": (left["y"], right["y"]), "recv": (far, far)}[kind]
            refs = [root.at[core, pl.ds(half * way, half), a] for way, a in enumerate(at)]
        for way, target in enumerate((right, left)):
            yield remote(
                refs[way], refs[way], root_ring_send.at[step, way], root_ring_recv.at[step, way],
                trade=trade_index(target),
            )

    def twin_copy(by, from_core):
        ref = root.at[from_core, :, (place["y"] + by) % NY]
        return remote(ref, ref, twin_send.at[by], twin_recv.at[by], scen=twin)

    weight[...] = jnp.where(
        lax.broadcasted_iota(jnp.int32, (1, positions), 1) < live_ref[...],
        principal_ref[...], 0.0,
    )

    own_draws.wait()
    for by in range(1, NY):
        draw_copy(by, (place["y"] + NY - by) % NY).wait_recv()
    def draw_start(step, part):
        for copy in draw_ring(step, "send", part):
            copy.start()

    def draw_advance(step, part):
        for date, plan in reversed(list(enumerate(draw_plans))):
            hand_on(
                draw_ring(step - 1, "recv", part, date), draw_ring(step, "send", part, date),
                plan[step][0][0][1] is not None,
            )

    def draw_arrived(step, part):
        for copy in draw_ring(step, "recv", part):
            copy.wait_recv()

    for part in range(HALVES):
        draw_start(0, part)

    for kind in range(2):
        @pl.when(zx < kinds[kind][1])
        def _(kind=kind):
            own_root(kind).wait()

        @pl.loop(0, NZ * NX)
        def _(source, kind=kind):
            @pl.when(jnp.logical_and(source < kinds[kind][1], source != zx))
            def _():
                root_copy(kind, zx, source).wait_recv()
    for copy in root_ring(0, "send"):
        copy.start()
    twin_copy(0, core).start()

    for part in range(HALVES):
        draw_advance(1, part)

    for copy in root_ring(0, "recv"):
        copy.wait_recv()
    for copy in root_ring(1, "send"):
        copy.start()
    twin_copy(1, core).start()
    twin_copy(3, core).start()

    for part in range(HALVES):
        draw_advance(2, part)

    for copy in root_ring(1, "recv"):
        copy.wait_recv()
    twin_copy(2, core).start()

    @pl.loop(0, positions // TILE)
    def _(tile):
        at = pl.ds(pl.multiple_of(tile * TILE, TILE), TILE)
        labels = lax.broadcasted_iota(jnp.int32, (sets, TILE), 0)
        member[:, at] = (labels == group_ref[:, at]).astype(F32).astype(BF16)

    for by in range(NY):
        twin_copy(by, 1 - core).wait_recv()

    dates = draws.shape[3]
    part_rows = span // CHUNKS

    def make_levels(part):
        rows = span // HALVES
        for col in range(COLS):
            home, slot = column_home(col)
            sources = [(s, y) for s in range(2 * (col + 1)) for y in range(NY)]
            left = jnp.concatenate(
                [
                    draws[s // NX, s % NX, y, :, pl.ds(part * rows, rows), :].reshape(dates * rows, LANES)
                    for s, y in sources
                ],
                axis=1,
            )
            right = jnp.concatenate([root[home, slot + s, y] for s, y in sources], axis=0)
            shocks = jnp.dot(left, right, preferred_element_type=F32)
            pull = pull_ref[pl.ds(factor_block(col, zx), 1), :]
            state = jnp.zeros((rows, LANES), F32)
            for date in range(dates):
                state = pull * state + shocks[date * rows:(date + 1) * rows]
                levels = state.astype(BF16)
                for chunk in range(CHUNKS // HALVES):
                    book[
                        part * (CHUNKS // HALVES) + chunk, place["z"], place["x"], col, place["y"],
                        pl.ds(date * part_rows, part_rows), :,
                    ] = levels[chunk * part_rows:(chunk + 1) * part_rows]

    plans = [part_steps(place, order) for _, _, order in PARTS]

    def view(part, chunk, coords, half):
        (col, cols), (row, rows), _ = PARTS[part]
        if half is not None:
            rows = rows // 2
            row = row + half * rows
        pick = [slice(None) if coords[a] is None else coords[a] for a in "zxy"]
        return book.at[chunk, pick[0], pick[1], pl.ds(col, cols), pick[2], pl.ds(row, rows), :]

    def descriptors(part, step, chunk, kind):
        sends, recvs = plans[part][step]
        for way in range(len(sends)):
            if kind == "send":
                coords, half, target = sends[way]
            else:
                coords, half = recvs[way]
                target = place
            ref = view(part, chunk, coords, half)
            yield remote(
                ref, ref, send_sems.at[chunk, part, step, way], recv_sems.at[chunk, part, step, way],
                trade=trade_index(target),
            )

    def start(chunk):
        for part in range(len(PARTS)):
            for copy in descriptors(part, 0, chunk, "send"):
                copy.start()

    def advance(step, chunk):
        for part in range(len(PARTS)):
            hand_on(
                descriptors(part, step - 1, chunk, "recv"), descriptors(part, step, chunk, "send"),
                plans[part][step][0][0][1] is not None,
            )

    def complete(chunk):
        for part in range(len(PARTS)):
            for copy in descriptors(part, STEPS - 1, chunk, "recv"):
                copy.wait_recv()

    half_chunks = CHUNKS // HALVES

    def both(part, act):
        @pl.loop(part * half_chunks, (part + 1) * half_chunks)
        def _(chunk):
            act(chunk)

    draw_arrived(2, 0)
    make_levels(0)
    both(0, start)
    both(0, functools.partial(advance, 1))
    draw_arrived(2, 1)
    make_levels(1)
    both(1, start)
    both(0, functools.partial(advance, 2))
    both(1, functools.partial(advance, 1))
    advance(3, 0)
    advance(2, 2)
    advance(3, 1)
    advance(2, 3)

    @pl.loop(0, CHUNKS - 2)
    def _(chunk):
        advance(4, chunk)
        advance(3, chunk + 2)

    def net_copy(chunk, target):
        return remote(
            net_out.at[chunk, target], net_in.at[chunk, me],
            net_send_sem, net_recv_sems.at[chunk], trade=target,
        )

    def compute(chunk):
        net[...] = jnp.zeros_like(net)
        levels = jnp.concatenate(
            [
                book[chunk, owner // NX, owner % NX, col].reshape(NY * ROWS, LANES)
                for col in range(COLS) for owner in range(NZ * NX)[:: 1 - 2 * (col % 2)]
            ],
            axis=1,
        )

        def strip(tile):
            return pl.ds(pl.multiple_of(tile * TILE, TILE), TILE)

        def price(tile, slot):
            prices[slot] = jnp.dot(levels, sens[:, strip(tile)], preferred_element_type=F32)

        def settle(tile, slot):
            at = strip(tile)
            values = weight[:, at] * softplus(prices[slot] + shift_ref[:, at])
            net[...] += lax.dot_general(
                member[:, at], values.astype(BF16), (((1,), (1,)), ((), ())),
                preferred_element_type=F32,
            )

        tiles = positions // TILE
        price(0, 0)

        @pl.loop(0, tiles // 2 - 1)
        def _(pair):
            price(2 * pair + 1, 1)
            settle(2 * pair, 0)
            price(2 * pair + 2, 0)
            settle(2 * pair + 1, 1)

        price(tiles - 1, 1)
        settle(tiles - 2, 0)
        settle(tiles - 1, 1)

        net_out[chunk] = net[...].astype(BF16).reshape(N_TRADE, SETS_DEV, NY * ROWS)

        @pl.loop(1, N_TRADE)
        def _(step):
            net_copy(chunk, (me + step) % N_TRADE).start()

        net_in[chunk, me] = net_out[chunk, me]

    fetch.wait()

    @pl.loop(0, CHUNKS)
    def _(chunk):
        @pl.when(chunk == 1)
        def _():
            advance(4, CHUNKS - 2)
            advance(4, CHUNKS - 1)

        complete(chunk)
        compute(chunk)

    for by in range(1, NY):
        draw_copy(by, place["y"]).wait_send()
    for part in range(HALVES):
        for step in range(DRAW_STEPS):
            for copy in draw_ring(step, "send", part):
                copy.wait_send()
    for kind in range(2):
        @pl.when(zx < kinds[kind][1])
        def _(kind=kind):
            @pl.loop(1, NZ * NX)
            def _(step):
                root_copy(kind, (zx + step) % (NZ * NX), zx).wait_send()
    for step in range(2):
        for copy in root_ring(step, "send"):
            copy.wait_send()
    for by in range(NY):
        twin_copy(by, core).wait_send()

    @pl.loop(0, CHUNKS)
    def _(chunk):
        for part in range(len(PARTS)):
            for step in range(STEPS):
                for copy in descriptors(part, step, chunk, "send"):
                    copy.wait_send()

    @pl.loop(0, CHUNKS)
    def _(chunk):
        whole = remote(
            net_out.at[chunk, pl.ds(0, N_TRADE - 1)], net_in.at[chunk, pl.ds(0, N_TRADE - 1)],
            net_send_sem, net_recv_sems.at[chunk], trade=me,
        )
        whole.wait_send()
        whole.wait_recv()
        total = jnp.zeros((SETS_DEV, NY * ROWS), F32)
        for sender in range(N_TRADE):
            total = total + net_in[chunk, sender].astype(F32)
        net[pl.ds(pl.multiple_of(chunk * SETS_DEV, SETS_DEV), SETS_DEV), :] = jnp.maximum(total, 0.0)

    mean_in[scen] = jnp.zeros(mean_in.shape[1:], F32)
    down = lax.broadcasted_iota(jnp.int32, (SETS_DEV, LANES), 0)
    across = lax.broadcasted_iota(jnp.int32, (SETS_DEV, LANES), 1)
    for date in range(dates):
        strip = jnp.concatenate(
            [
                net[chunk * SETS_DEV:(chunk + 1) * SETS_DEV, y * ROWS + date * part_rows:][:, :part_rows]
                for y in range(NY) for chunk in range(CHUNKS)
            ],
            axis=1,
        )
        out_ref[date] = strip
        sums = jnp.where(down == across, jnp.sum(strip, axis=1, keepdims=True), 0.0)
        mean_in[scen, pl.ds(date, 1), :] = jnp.sum(sums, axis=0, keepdims=True)

    def mean_copy(by, slot):
        return remote(
            mean_in.at[slot], mean_in.at[slot], mean_send.at[by - 1], mean_recv.at[by - 1],
            scen=(scen + by) % scens,
        )

    for by in range(1, scens):
        mean_copy(by, scen).start()

    for by in range(1, scens):
        mean_copy(by, (scen + scens - by) % scens).wait_recv()
        mean_copy(by, scen).wait_send()
    total = jnp.sum(mean_in[...], axis=0) / (scens * NY * span)
    mean_ref[...] = total[:dates, :SETS_DEV]


def exposures(draws, root, sensitivity, pull, shift, principal, group, live):
    dates, scen, _ = draws.shape
    positions = sensitivity.shape[1]
    sets = SETS_DEV * N_TRADE
    span = scen // NY
    vmem = pl.BlockSpec(memory_space=pltpu.VMEM)
    hbm = pl.BlockSpec(memory_space=pl.ANY)
    dma = pltpu.SemaphoreType.DMA
    return pl.pallas_call(
        exposure_kernel,
        out_shape=(
            jax.ShapeDtypeStruct((dates, SETS_DEV, scen), F32),
            jax.ShapeDtypeStruct((dates, SETS_DEV), F32),
        ),
        in_specs=[hbm, hbm, hbm, vmem, vmem, vmem, vmem, vmem],
        out_specs=(vmem, vmem),
        scratch_shapes=[
            pltpu.VMEM((NZ, NX, NY, dates, span, LANES), BF16),
            pltpu.VMEM((2, SLOTS, NY, LANES, LANES), BF16),
            pltpu.VMEM((CHUNKS, NZ, NX, COLS, NY, ROWS, LANES), BF16),
            pltpu.VMEM(sensitivity.shape, BF16),
            pltpu.VMEM((sets, positions), BF16),
            pltpu.VMEM((1, positions), F32),
            pltpu.VMEM((sets, NY * ROWS), F32),
            pltpu.VMEM((2, NY * ROWS, TILE), F32),
            pltpu.VMEM((CHUNKS, N_TRADE, SETS_DEV, NY * ROWS), BF16),
            pltpu.VMEM((CHUNKS, N_TRADE, SETS_DEV, NY * ROWS), BF16),
            pltpu.VMEM((lax.axis_size("scen"), 8, LANES), F32),
            dma((NY - 1,)), dma((NY - 1,)),
            dma((HALVES, dates, DRAW_STEPS, 2)), dma((HALVES, dates, DRAW_STEPS, 2)),
            dma((2, NZ * NX)), dma((2, NZ * NX)),
            dma((2, 2)), dma((2, 2)), dma((NY,)), dma((NY,)),
            dma((CHUNKS, len(PARTS), STEPS, 2)), dma((CHUNKS, len(PARTS), STEPS, 2)),
            dma((3,)), dma, dma, dma((CHUNKS,)),
            dma((lax.axis_size("scen") - 1,)), dma((lax.axis_size("scen") - 1,)),
        ],
        compiler_params=pltpu.CompilerParams(
            collective_id=1, has_side_effects=True, vmem_limit_bytes=58 * 2**20
        ),
        cost_estimate=pl.CostEstimate(
            flops=2 * 1024 * positions * (4096 + sets), bytes_accessed=17 << 20, transcendentals=0
        ),
        name="exposures",
    )(
        draws, root, sensitivity, pull.reshape(-1, LANES), shift.reshape(1, -1),
        principal.reshape(1, -1), group.reshape(1, -1), live.reshape(1, 1),
    )


def on_device(
    normal_draws, covariance_root, mean_pullback, sensitivity_tensor,
    moneyness_shift, signed_principal, deal_agreement_group, active_position_number,
):
    exposure, mean = exposures(
        normal_draws, covariance_root, sensitivity_tensor, mean_pullback, moneyness_shift,
        signed_principal, deal_agreement_group, active_position_number,
    )
    return exposure.transpose(0, 2, 1), mean


def solution(mesh):
    in_specs = (
        P(None, "scen", "trade"), P("trade", None), P(), P(None, "trade"),
        P("trade"), P("trade"), P("trade"), P("trade"),
    )
    out_specs = (P(None, "scen", "trade"), P(None, "trade"))
    return jax.shard_map(
        on_device, mesh=mesh, in_specs=in_specs, out_specs=out_specs, check_vma=False
    )
```

```python
import functools
import jax
import jax.numpy as jnp
from jax import lax
from jax.experimental import pallas as pl
from jax.experimental.pallas import tpu as pltpu
from jax.sharding import PartitionSpec as P

F32, BF16 = jnp.float32, jnp.bfloat16
SETS_DEV = 16
NZ, NX, NY = 2, 4, 4
N_TRADE = NZ * NX * NY
CHUNKS = 4
COLS = 4
ROWS = 64
LANES = 128
TILE = 512
HALVES = 2
PARTS = (
    ((0, 3), (0, 32), ("z", "y", "x")),
    ((0, 3), (32, 32), ("z", "x", "y")),
    ((3, 1), (0, 32), ("x", "y", "z")),
    ((3, 1), (32, 32), ("y", "x", "z")),
)
STEPS = 5
DRAW_ORDERS = (("z", "x"), ("x", "z"))
DRAW_STEPS = 3
SLOTS = 10


def trade_place():
    me = lax.axis_index("trade")
    return {"z": me // (NX * NY), "x": (me // NY) % NX, "y": me % NY}


def trade_index(place):
    return (place["z"] * NX + place["x"]) * NY + place["y"]


def moved(place, axis, by):
    size = {"z": NZ, "x": NX, "y": NY}[axis]
    return dict(place, **{axis: (place[axis] + by) % size})


def part_steps(place, order):
    have = dict(place)
    steps = []
    for axis in order:
        if axis == "z":
            steps.append(
                (
                    [(dict(have), None, moved(place, "z", 1))],
                    [(dict(have, z=1 - place["z"]), None)],
                )
            )
        else:
            right, left = moved(place, axis, 1), moved(place, axis, 3)
            far = moved(place, axis, 2)
            at = lambda where: dict(have, **{axis: where[axis]})
            steps.append(
                (
                    [(at(place), None, right), (at(place), None, left)],
                    [(at(left), None), (at(right), None)],
                )
            )
            steps.append(
                (
                    [(at(left), 0, right), (at(right), 1, left)],
                    [(at(far), 0), (at(far), 1)],
                )
            )
        have[axis] = None
    return steps


def hand_on(arrivals, sends, pairwise):
    arrivals, sends = list(arrivals), list(sends)
    if pairwise:
        for arrival, send in zip(arrivals, sends):
            arrival.wait_recv()
            send.start()
    else:
        for arrival in arrivals:
            arrival.wait_recv()
        for send in sends:
            send.start()


def softplus(a):
    return jnp.maximum(a, 0.0) + jnp.log(1.0 + jnp.exp(-jnp.abs(a)))


def factor_block(col, owner):
    return 8 * col + (owner if col % 2 == 0 else 7 - owner)


def column_home(col):
    return {3: (0, 0), 0: (0, 8), 2: (1, 0), 1: (1, 6)}[col]


def exposure_kernel(
    draws_hbm, root_hbm, sens_hbm, pull_ref, shift_ref, principal_ref, group_ref, live_ref,
    out_ref, mean_ref,
    draws, root, book, sens, member, weight, net, prices, net_out, net_in, mean_in,
    draw_send, draw_recv, draw_ring_send, draw_ring_recv,
    root_send, root_recv, root_ring_send, root_ring_recv, twin_send, twin_recv,
    send_sems, recv_sems, own_sems, sens_sem, net_send_sems, net_recv_sems,
    mean_send, mean_recv,
):
    place = trade_place()
    me = trade_index(place)
    zx = place["z"] * NX + place["x"]
    scen = lax.axis_index("scen")
    scens = lax.axis_size("scen")
    core = scen % 2
    twin = scen + 1 - 2 * core
    positions = sens.shape[1]
    sets = member.shape[0]
    span = draws_hbm.shape[1] // NY

    def remote(src, dst, send, recv, **target):
        return pltpu.make_async_remote_copy(
            src_ref=src, dst_ref=dst, send_sem=send, recv_sem=recv,
            device_id=target, device_id_type=pl.DeviceIdType.MESH,
        )

    barrier = pltpu.get_barrier_semaphore()

    @pl.loop(1, N_TRADE)
    def _(step):
        pl.semaphore_signal(
            barrier, inc=1, device_id={"trade": (me + step) % N_TRADE},
            device_id_type=pl.DeviceIdType.MESH,
        )

    @pl.loop(1, scens)
    def _(step):
        pl.semaphore_signal(
            barrier, inc=1, device_id={"scen": (scen + step) % scens},
            device_id_type=pl.DeviceIdType.MESH,
        )

    pl.semaphore_wait(barrier, N_TRADE - 1 + scens - 1)

    def draw_rows(y):
        return draws_hbm.at[:, pl.ds(y * span, span), :]

    def draw_copy(by, source):
        return remote(
            draw_rows((place["y"] + by) % NY), draws.at[place["z"], place["x"], source],
            draw_send.at[by - 1], draw_recv.at[by - 1],
            trade=trade_index(moved(place, "y", by)),
        )

    own_draws = pltpu.make_async_copy(
        draw_rows(place["y"]), draws.at[place["z"], place["x"], place["y"]], own_sems.at[0]
    )
    own_draws.start()
    for by in range(1, NY):
        draw_copy(by, place["y"]).start()

    high_count, low_count = 8 - 2 * core, 2 + 2 * core
    kinds = ((3 - core, high_count, 0), (core, low_count, high_count))

    def root_block(kind, owner):
        col = kinds[kind][0]
        block = 8 * col + jnp.where(col % 2 == 0, owner, 7 - owner)
        return root_hbm.at[:, pl.ds(pl.multiple_of(block * LANES, LANES), LANES)]

    def root_slot(kind, source):
        return root.at[core, kinds[kind][2] + source, place["y"]]

    def root_copy(kind, owner, source):
        return remote(
            root_block(kind, owner), root_slot(kind, source),
            root_send.at[kind, owner], root_recv.at[kind, source],
            trade=owner * NY + place["y"],
        )

    def own_root(kind):
        return pltpu.make_async_copy(root_block(kind, zx), root_slot(kind, zx), own_sems.at[1 + kind])

    for kind in range(2):
        @pl.when(zx < kinds[kind][1])
        def _(kind=kind):
            own_root(kind).start()

            @pl.loop(1, NZ * NX)
            def _(step):
                root_copy(kind, (zx + step) % (NZ * NX), zx).start()

    fetch = pltpu.make_async_copy(sens_hbm, sens, sens_sem)
    fetch.start()

    draw_plans = [part_steps(place, order) for order in DRAW_ORDERS]

    def draw_ring(step, kind, part, only=None):
        for date, plan in reversed(list(enumerate(draw_plans))):
            if only is not None and date != only:
                continue
            sends, recvs = plan[step]
            for way in range(len(sends)):
                coords, half = (sends if kind == "send" else recvs)[way][:2]
                target = sends[way][2]
                rows = span // HALVES
                row = part * rows
                if half is not None:
                    rows = rows // 2
                    row = row + half * rows
                pick = [slice(None) if coords[a] is None else coords[a] for a in "zx"]
                ref = draws.at[pick[0], pick[1], :, date, pl.ds(row, rows), :]
                yield remote(
                    ref, ref, draw_ring_send.at[part, date, step, way],
                    draw_ring_recv.at[part, date, step, way],
                    trade=trade_index(target),
                )

    def root_ring(step, kind):
        y = place["y"]
        right, left = moved(place, "y", 1), moved(place, "y", 3)
        far = (y + 2) % NY
        half = SLOTS // 2
        if step == 0:
            at = {"send": (y, y), "recv": (left["y"], right["y"])}[kind]
            refs = [root.at[core, :, a] for a in at]
        else:
            at = {"send": (left["y"], right["y"]), "recv": (far, far)}[kind]
            refs = [root.at[core, pl.ds(half * way, half), a] for way, a in enumerate(at)]
        for way, target in enumerate((right, left)):
            yield remote(
                refs[way], refs[way], root_ring_send.at[step, way], root_ring_recv.at[step, way],
                trade=trade_index(target),
            )

    def twin_copy(by, from_core):
        ref = root.at[from_core, :, (place["y"] + by) % NY]
        return remote(ref, ref, twin_send.at[by], twin_recv.at[by], scen=twin)

    own_draws.wait()
    for by in range(1, NY):
        draw_copy(by, (place["y"] + NY - by) % NY).wait_recv()
    def draw_start(step, part):
        for copy in draw_ring(step, "send", part):
            copy.start()

    def draw_advance(step, part):
        for date, plan in reversed(list(enumerate(draw_plans))):
            hand_on(
                draw_ring(step - 1, "recv", part, date), draw_ring(step, "send", part, date),
                plan[step][0][0][1] is not None,
            )

    def draw_arrived(step, part):
        for copy in draw_ring(step, "recv", part):
            copy.wait_recv()

    for part in range(HALVES):
        draw_start(0, part)

    for kind in range(2):
        @pl.when(zx < kinds[kind][1])
        def _(kind=kind):
            own_root(kind).wait()

        @pl.loop(0, NZ * NX)
        def _(source, kind=kind):
            @pl.when(jnp.logical_and(source < kinds[kind][1], source != zx))
            def _():
                root_copy(kind, zx, source).wait_recv()
    for copy in root_ring(0, "send"):
        copy.start()
    twin_copy(0, core).start()

    for part in range(HALVES):
        draw_advance(1, part)

    hand_on(root_ring(0, "recv"), root_ring(1, "send"), True)
    twin_copy(1, core).start()
    twin_copy(3, core).start()

    for part in range(HALVES):
        draw_advance(2, part)

    for copy in root_ring(1, "recv"):
        copy.wait_recv()
    twin_copy(2, core).start()

    for by in range(NY):
        twin_copy(by, 1 - core).wait_recv()

    dates = draws.shape[3]
    part_rows = span // CHUNKS

    def make_levels(part):
        rows = span // HALVES
        for col in range(COLS):
            home, slot = column_home(col)
            sources = [(s, y) for s in range(2 * (col + 1)) for y in range(NY)]
            left = jnp.concatenate(
                [
                    draws[s // NX, s % NX, y, :, pl.ds(part * rows, rows), :].reshape(dates * rows, LANES)
                    for s, y in sources
                ],
                axis=1,
            )
            right = jnp.concatenate([root[home, slot + s, y] for s, y in sources], axis=0)
            shocks = jnp.dot(left, right, preferred_element_type=F32)
            pull = pull_ref[pl.ds(factor_block(col, zx), 1), :]
            state = jnp.zeros((rows, LANES), F32)
            for date in range(dates):
                state = pull * state + shocks[date * rows:(date + 1) * rows]
                levels = state.astype(BF16)
                for chunk in range(CHUNKS // HALVES):
                    book[
                        part * (CHUNKS // HALVES) + chunk, place["z"], place["x"], col, place["y"],
                        pl.ds(date * part_rows, part_rows), :,
                    ] = levels[chunk * part_rows:(chunk + 1) * part_rows]

    plans = [part_steps(place, order) for _, _, order in PARTS]

    def view(part, chunk, coords, half):
        (col, cols), (row, rows), _ = PARTS[part]
        if half is not None:
            rows = rows // 2
            row = row + half * rows
        pick = [slice(None) if coords[a] is None else coords[a] for a in "zxy"]
        return book.at[chunk, pick[0], pick[1], pl.ds(col, cols), pick[2], pl.ds(row, rows), :]

    def descriptors(part, step, chunk, kind):
        sends, recvs = plans[part][step]
        for way in range(len(sends)):
            if kind == "send":
                coords, half, target = sends[way]
            else:
                coords, half = recvs[way]
                target = place
            ref = view(part, chunk, coords, half)
            yield remote(
                ref, ref, send_sems.at[chunk, part, step, way], recv_sems.at[chunk, part, step, way],
                trade=trade_index(target),
            )

    def start(chunk):
        for part in range(len(PARTS)):
            for copy in descriptors(part, 0, chunk, "send"):
                copy.start()

    def advance(step, chunk):
        for part in range(len(PARTS)):
            hand_on(
                descriptors(part, step - 1, chunk, "recv"), descriptors(part, step, chunk, "send"),
                plans[part][step][0][0][1] is not None,
            )

    def complete(chunk):
        for part in range(len(PARTS)):
            for copy in descriptors(part, STEPS - 1, chunk, "recv"):
                copy.wait_recv()

    half_chunks = CHUNKS // HALVES

    def both(part, act):
        @pl.loop(part * half_chunks, (part + 1) * half_chunks)
        def _(chunk):
            act(chunk)

    draw_arrived(2, 0)
    make_levels(0)
    both(0, start)
    both(0, functools.partial(advance, 1))
    draw_arrived(2, 1)
    make_levels(1)
    both(1, start)
    both(0, functools.partial(advance, 2))
    both(1, functools.partial(advance, 1))
    advance(3, 0)
    advance(2, 2)
    advance(3, 1)
    advance(2, 3)

    @pl.loop(0, CHUNKS - 2)
    def _(chunk):
        advance(4, chunk)
        advance(3, chunk + 2)

    def net_copy(late, target):
        first, count = ((0, CHUNKS - 1), (CHUNKS - 1, 1))[late]
        return remote(
            net_out.at[target, pl.ds(first, count)], net_in.at[me, pl.ds(first, count)],
            net_send_sems.at[late], net_recv_sems.at[late], trade=target,
        )

    def send_nets(late):
        @pl.loop(1, N_TRADE)
        def _(step):
            net_copy(late, (me + step) % N_TRADE).start()

    def await_nets(late):
        first, count = ((0, CHUNKS - 1), (CHUNKS - 1, 1))[late]
        whole = remote(
            net_out.at[pl.ds(0, N_TRADE - 1), pl.ds(first, count)],
            net_in.at[pl.ds(0, N_TRADE - 1), pl.ds(first, count)],
            net_send_sems.at[late], net_recv_sems.at[late], trade=me,
        )
        whole.wait_send()
        whole.wait_recv()

    def add_nets(chunk):
        total = jnp.zeros((SETS_DEV, NY * ROWS), F32)
        for sender in range(N_TRADE):
            total = total + net_in[sender, chunk].astype(F32)
        net[pl.ds(pl.multiple_of(chunk * SETS_DEV, SETS_DEV), SETS_DEV), :] = jnp.maximum(total, 0.0)

    def compute(chunk):
        net[...] = jnp.zeros_like(net)
        levels = jnp.concatenate(
            [
                book[chunk, owner // NX, owner % NX, col].reshape(NY * ROWS, LANES)
                for col in range(COLS) for owner in range(NZ * NX)[:: 1 - 2 * (col % 2)]
            ],
            axis=1,
        )

        def strip(tile):
            return pl.ds(pl.multiple_of(tile * TILE, TILE), TILE)

        def price(tile, slot):
            prices[slot] = jnp.dot(levels, sens[:, strip(tile)], preferred_element_type=F32)

        def settle(tile, slot):
            at = strip(tile)
            values = weight[:, at] * softplus(prices[slot] + shift_ref[:, at])
            net[...] += lax.dot_general(
                member[:, at], values.astype(BF16), (((1,), (1,)), ((), ())),
                preferred_element_type=F32,
            )

        tiles = positions // TILE
        price(0, 0)

        @pl.loop(0, tiles // 2 - 1)
        def _(pair):
            price(2 * pair + 1, 1)
            settle(2 * pair, 0)
            price(2 * pair + 2, 0)
            settle(2 * pair + 1, 1)

        price(tiles - 1, 1)
        settle(tiles - 2, 0)
        settle(tiles - 1, 1)

        for owner in range(N_TRADE):
            net_out[owner, chunk] = net[owner * SETS_DEV:(owner + 1) * SETS_DEV].astype(BF16)
        net_in[me, chunk] = net_out[me, chunk]

    weight[...] = jnp.where(
        lax.broadcasted_iota(jnp.int32, (1, positions), 1) < live_ref[...],
        principal_ref[...], 0.0,
    )

    @pl.loop(0, positions // TILE)
    def _(tile):
        at = pl.ds(pl.multiple_of(tile * TILE, TILE), TILE)
        labels = lax.broadcasted_iota(jnp.int32, (sets, TILE), 0)
        member[:, at] = (labels == group_ref[:, at]).astype(F32).astype(BF16)

    fetch.wait()

    @pl.loop(0, CHUNKS)
    def _(chunk):
        @pl.when(chunk == 1)
        def _():
            advance(4, CHUNKS - 2)
            advance(4, CHUNKS - 1)

        complete(chunk)

        @pl.when(chunk == CHUNKS - 1)
        def _():
            send_nets(0)

        compute(chunk)

    send_nets(1)

    for by in range(1, NY):
        draw_copy(by, place["y"]).wait_send()
    for part in range(HALVES):
        for step in range(DRAW_STEPS):
            for copy in draw_ring(step, "send", part):
                copy.wait_send()
    for kind in range(2):
        @pl.when(zx < kinds[kind][1])
        def _(kind=kind):
            @pl.loop(1, NZ * NX)
            def _(step):
                root_copy(kind, (zx + step) % (NZ * NX), zx).wait_send()
    for step in range(2):
        for copy in root_ring(step, "send"):
            copy.wait_send()
    for by in range(NY):
        twin_copy(by, core).wait_send()

    @pl.loop(0, CHUNKS)
    def _(chunk):
        for part in range(len(PARTS)):
            for step in range(STEPS):
                for copy in descriptors(part, step, chunk, "send"):
                    copy.wait_send()

    await_nets(0)

    @pl.loop(0, CHUNKS - 1)
    def _(chunk):
        add_nets(chunk)

    await_nets(1)
    add_nets(CHUNKS - 1)

    mean_in[scen] = jnp.zeros(mean_in.shape[1:], F32)
    down = lax.broadcasted_iota(jnp.int32, (SETS_DEV, LANES), 0)
    across = lax.broadcasted_iota(jnp.int32, (SETS_DEV, LANES), 1)
    for date in range(dates):
        strip = jnp.concatenate(
            [
                net[chunk * SETS_DEV:(chunk + 1) * SETS_DEV, y * ROWS + date * part_rows:][:, :part_rows]
                for y in range(NY) for chunk in range(CHUNKS)
            ],
            axis=1,
        )
        out_ref[date] = strip
        sums = jnp.where(down == across, jnp.sum(strip, axis=1, keepdims=True), 0.0)
        mean_in[scen, pl.ds(date, 1), :] = jnp.sum(sums, axis=0, keepdims=True)

    def mean_copy(by, slot):
        return remote(
            mean_in.at[slot], mean_in.at[slot], mean_send.at[by - 1], mean_recv.at[by - 1],
            scen=(scen + by) % scens,
        )

    for by in range(1, scens):
        mean_copy(by, scen).start()

    for by in range(1, scens):
        mean_copy(by, (scen + scens - by) % scens).wait_recv()
        mean_copy(by, scen).wait_send()
    total = jnp.sum(mean_in[...], axis=0) / (scens * NY * span)
    mean_ref[...] = total[:dates, :SETS_DEV]


def exposures(draws, root, sensitivity, pull, shift, principal, group, live):
    dates, scen, _ = draws.shape
    positions = sensitivity.shape[1]
    sets = SETS_DEV * N_TRADE
    span = scen // NY
    vmem = pl.BlockSpec(memory_space=pltpu.VMEM)
    hbm = pl.BlockSpec(memory_space=pl.ANY)
    dma = pltpu.SemaphoreType.DMA
    return pl.pallas_call(
        exposure_kernel,
        out_shape=(
            jax.ShapeDtypeStruct((dates, SETS_DEV, scen), F32),
            jax.ShapeDtypeStruct((dates, SETS_DEV), F32),
        ),
        in_specs=[hbm, hbm, hbm, vmem, vmem, vmem, vmem, vmem],
        out_specs=(vmem, vmem),
        scratch_shapes=[
            pltpu.VMEM((NZ, NX, NY, dates, span, LANES), BF16),
            pltpu.VMEM((2, SLOTS, NY, LANES, LANES), BF16),
            pltpu.VMEM((CHUNKS, NZ, NX, COLS, NY, ROWS, LANES), BF16),
            pltpu.VMEM(sensitivity.shape, BF16),
            pltpu.VMEM((sets, positions), BF16),
            pltpu.VMEM((1, positions), F32),
            pltpu.VMEM((sets, NY * ROWS), F32),
            pltpu.VMEM((2, NY * ROWS, TILE), F32),
            pltpu.VMEM((N_TRADE, CHUNKS, SETS_DEV, NY * ROWS), BF16),
            pltpu.VMEM((N_TRADE, CHUNKS, SETS_DEV, NY * ROWS), BF16),
            pltpu.VMEM((lax.axis_size("scen"), 8, LANES), F32),
            dma((NY - 1,)), dma((NY - 1,)),
            dma((HALVES, dates, DRAW_STEPS, 2)), dma((HALVES, dates, DRAW_STEPS, 2)),
            dma((2, NZ * NX)), dma((2, NZ * NX)),
            dma((2, 2)), dma((2, 2)), dma((NY,)), dma((NY,)),
            dma((CHUNKS, len(PARTS), STEPS, 2)), dma((CHUNKS, len(PARTS), STEPS, 2)),
            dma((3,)), dma, dma((2,)), dma((2,)),
            dma((lax.axis_size("scen") - 1,)), dma((lax.axis_size("scen") - 1,)),
        ],
        compiler_params=pltpu.CompilerParams(
            collective_id=1, has_side_effects=True, vmem_limit_bytes=58 * 2**20
        ),
        cost_estimate=pl.CostEstimate(
            flops=2 * 1024 * positions * (4096 + sets), bytes_accessed=17 << 20, transcendentals=0
        ),
        name="exposures",
    )(
        draws, root, sensitivity, pull.reshape(-1, LANES), shift.reshape(1, -1),
        principal.reshape(1, -1), group.reshape(1, -1), live.reshape(1, 1),
    )


def on_device(
    normal_draws, covariance_root, mean_pullback, sensitivity_tensor,
    moneyness_shift, signed_principal, deal_agreement_group, active_position_number,
):
    exposure, mean = exposures(
        normal_draws, covariance_root, sensitivity_tensor, mean_pullback, moneyness_shift,
        signed_principal, deal_agreement_group, active_position_number,
    )
    return exposure.transpose(0, 2, 1), mean


def solution(mesh):
    in_specs = (
        P(None, "scen", "trade"), P("trade", None), P(), P(None, "trade"),
        P("trade"), P("trade"), P("trade"), P("trade"),
    )
    out_specs = (P(None, "scen", "trade"), P(None, "trade"))
    return jax.shard_map(
        on_device, mesh=mesh, in_specs=in_specs, out_specs=out_specs, check_vma=False
    )
```

```python
import functools
import jax
import jax.numpy as jnp
from jax import lax
from jax.experimental import pallas as pl
from jax.experimental.pallas import tpu as pltpu
from jax.sharding import PartitionSpec as P

F32, BF16 = jnp.float32, jnp.bfloat16
SETS_DEV = 16
NZ, NX, NY = 2, 4, 4
N_TRADE = NZ * NX * NY
CHUNKS = 4
COLS = 4
ROWS = 64
LANES = 128
TILE = 512
HALVES = 2
PARTS = (
    ((0, 3), (0, 32), ("z", "y", "x")),
    ((0, 3), (32, 32), ("z", "x", "y")),
    ((3, 1), (0, 32), ("x", "y", "z")),
    ((3, 1), (32, 32), ("y", "x", "z")),
)
STEPS = 5
DRAW_ORDERS = (("z", "x"), ("x", "z"))
DRAW_STEPS = 3
SLOTS = 10
NET_GROUPS = ((0, CHUNKS - 2), (CHUNKS - 2, 1), (CHUNKS - 1, 1))


def trade_place():
    me = lax.axis_index("trade")
    return {"z": me // (NX * NY), "x": (me // NY) % NX, "y": me % NY}


def trade_index(place):
    return (place["z"] * NX + place["x"]) * NY + place["y"]


def moved(place, axis, by):
    size = {"z": NZ, "x": NX, "y": NY}[axis]
    return dict(place, **{axis: (place[axis] + by) % size})


def part_steps(place, order):
    have = dict(place)
    steps = []
    for axis in order:
        if axis == "z":
            steps.append(
                (
                    [(dict(have), None, moved(place, "z", 1))],
                    [(dict(have, z=1 - place["z"]), None)],
                )
            )
        else:
            right, left = moved(place, axis, 1), moved(place, axis, 3)
            far = moved(place, axis, 2)
            at = lambda where: dict(have, **{axis: where[axis]})
            steps.append(
                (
                    [(at(place), None, right), (at(place), None, left)],
                    [(at(left), None), (at(right), None)],
                )
            )
            steps.append(
                (
                    [(at(left), 0, right), (at(right), 1, left)],
                    [(at(far), 0), (at(far), 1)],
                )
            )
        have[axis] = None
    return steps


def hand_on(arrivals, sends, pairwise):
    arrivals, sends = list(arrivals), list(sends)
    if pairwise:
        for arrival, send in zip(arrivals, sends):
            arrival.wait_recv()
            send.start()
    else:
        for arrival in arrivals:
            arrival.wait_recv()
        for send in sends:
            send.start()


def softplus(a):
    return jnp.maximum(a, 0.0) + jnp.log(1.0 + jnp.exp(-jnp.abs(a)))


def factor_block(col, owner):
    return 8 * col + (owner if col % 2 == 0 else 7 - owner)


def column_home(col):
    return {3: (0, 0), 0: (0, 8), 2: (1, 0), 1: (1, 6)}[col]


def exposure_kernel(
    draws_hbm, root_hbm, sens_hbm, pull_ref, shift_ref, principal_ref, group_ref, live_ref,
    out_ref, mean_ref,
    draws, root, book, sens, member, weight, net, prices, net_out, net_in, mean_in,
    draw_send, draw_recv, draw_ring_send, draw_ring_recv,
    root_send, root_recv, root_ring_send, root_ring_recv, twin_send, twin_recv,
    send_sems, recv_sems, own_sems, sens_sem, net_send_sems, net_recv_sems,
    mean_send, mean_recv,
):
    place = trade_place()
    me = trade_index(place)
    zx = place["z"] * NX + place["x"]
    scen = lax.axis_index("scen")
    scens = lax.axis_size("scen")
    core = scen % 2
    twin = scen + 1 - 2 * core
    positions = sens.shape[1]
    sets = member.shape[0]
    span = draws_hbm.shape[1] // NY

    def remote(src, dst, send, recv, **target):
        return pltpu.make_async_remote_copy(
            src_ref=src, dst_ref=dst, send_sem=send, recv_sem=recv,
            device_id=target, device_id_type=pl.DeviceIdType.MESH,
        )

    barrier = pltpu.get_barrier_semaphore()

    @pl.loop(1, N_TRADE)
    def _(step):
        pl.semaphore_signal(
            barrier, inc=1, device_id={"trade": (me + step) % N_TRADE},
            device_id_type=pl.DeviceIdType.MESH,
        )

    @pl.loop(1, scens)
    def _(step):
        pl.semaphore_signal(
            barrier, inc=1, device_id={"scen": (scen + step) % scens},
            device_id_type=pl.DeviceIdType.MESH,
        )

    pl.semaphore_wait(barrier, N_TRADE - 1 + scens - 1)

    def draw_rows(y):
        return draws_hbm.at[:, pl.ds(y * span, span), :]

    def draw_copy(by, source):
        return remote(
            draw_rows((place["y"] + by) % NY), draws.at[place["z"], place["x"], source],
            draw_send.at[by - 1], draw_recv.at[by - 1],
            trade=trade_index(moved(place, "y", by)),
        )

    own_draws = pltpu.make_async_copy(
        draw_rows(place["y"]), draws.at[place["z"], place["x"], place["y"]], own_sems.at[0]
    )
    own_draws.start()
    for by in range(1, NY):
        draw_copy(by, place["y"]).start()

    high_count, low_count = 8 - 2 * core, 2 + 2 * core
    kinds = ((3 - core, high_count, 0), (core, low_count, high_count))

    def root_block(kind, owner):
        col = kinds[kind][0]
        block = 8 * col + jnp.where(col % 2 == 0, owner, 7 - owner)
        return root_hbm.at[:, pl.ds(pl.multiple_of(block * LANES, LANES), LANES)]

    def root_slot(kind, source):
        return root.at[core, kinds[kind][2] + source, place["y"]]

    def root_copy(kind, owner, source):
        return remote(
            root_block(kind, owner), root_slot(kind, source),
            root_send.at[kind, owner], root_recv.at[kind, source],
            trade=owner * NY + place["y"],
        )

    def own_root(kind):
        return pltpu.make_async_copy(root_block(kind, zx), root_slot(kind, zx), own_sems.at[1 + kind])

    for kind in range(2):
        @pl.when(zx < kinds[kind][1])
        def _(kind=kind):
            own_root(kind).start()

            @pl.loop(1, NZ * NX)
            def _(step):
                root_copy(kind, (zx + step) % (NZ * NX), zx).start()

    fetch = pltpu.make_async_copy(sens_hbm, sens, sens_sem)
    fetch.start()

    draw_plans = [part_steps(place, order) for order in DRAW_ORDERS]

    def draw_ring(step, kind, part, only=None):
        for date, plan in reversed(list(enumerate(draw_plans))):
            if only is not None and date != only:
                continue
            sends, recvs = plan[step]
            for way in range(len(sends)):
                coords, half = (sends if kind == "send" else recvs)[way][:2]
                target = sends[way][2]
                rows = span // HALVES
                row = part * rows
                if half is not None:
                    rows = rows // 2
                    row = row + half * rows
                pick = [slice(None) if coords[a] is None else coords[a] for a in "zx"]
                ref = draws.at[pick[0], pick[1], :, date, pl.ds(row, rows), :]
                yield remote(
                    ref, ref, draw_ring_send.at[part, date, step, way],
                    draw_ring_recv.at[part, date, step, way],
                    trade=trade_index(target),
                )

    def root_ring(step, kind):
        y = place["y"]
        right, left = moved(place, "y", 1), moved(place, "y", 3)
        far = (y + 2) % NY
        half = SLOTS // 2
        if step < 2:
            at = {"send": (y, y), "recv": (left["y"], right["y"])}[kind]
        else:
            at = {"send": (left["y"], right["y"]), "recv": (far, far)}[kind]
        refs = [
            root.at[core, pl.ds(half * (way if step != 1 else 1 - way), half), a]
            for way, a in enumerate(at)
        ]
        for way, target in enumerate((right, left)):
            yield remote(
                refs[way], refs[way], root_ring_send.at[step, way], root_ring_recv.at[step, way],
                trade=trade_index(target),
            )

    def twin_copy(by, from_core):
        ref = root.at[from_core, :, (place["y"] + by) % NY]
        return remote(ref, ref, twin_send.at[by], twin_recv.at[by], scen=twin)

    own_draws.wait()
    for by in range(1, NY):
        draw_copy(by, (place["y"] + NY - by) % NY).wait_recv()
    def draw_start(step, part):
        for copy in draw_ring(step, "send", part):
            copy.start()

    def draw_advance(step, part):
        for date, plan in reversed(list(enumerate(draw_plans))):
            hand_on(
                draw_ring(step - 1, "recv", part, date), draw_ring(step, "send", part, date),
                plan[step][0][0][1] is not None,
            )

    def draw_arrived(step, part):
        for copy in draw_ring(step, "recv", part):
            copy.wait_recv()

    for part in range(HALVES):
        draw_start(0, part)

    for kind in range(2):
        @pl.when(zx < kinds[kind][1])
        def _(kind=kind):
            own_root(kind).wait()

        @pl.loop(0, NZ * NX)
        def _(source, kind=kind):
            @pl.when(jnp.logical_and(source < kinds[kind][1], source != zx))
            def _():
                root_copy(kind, zx, source).wait_recv()
    for step in range(2):
        for copy in root_ring(step, "send"):
            copy.start()
    twin_copy(0, core).start()

    for part in range(HALVES):
        draw_advance(1, part)

    hand_on(root_ring(0, "recv"), root_ring(2, "send"), True)
    for copy in root_ring(1, "recv"):
        copy.wait_recv()
    twin_copy(1, core).start()
    twin_copy(3, core).start()

    for part in range(HALVES):
        draw_advance(2, part)

    for copy in root_ring(2, "recv"):
        copy.wait_recv()
    twin_copy(2, core).start()

    for by in range(NY):
        twin_copy(by, 1 - core).wait_recv()

    dates = draws.shape[3]
    part_rows = span // CHUNKS

    def make_levels(part):
        rows = span // HALVES
        for col in range(COLS):
            home, slot = column_home(col)
            sources = [(s, y) for s in range(2 * (col + 1)) for y in range(NY)]
            left = jnp.concatenate(
                [
                    draws[s // NX, s % NX, y, :, pl.ds(part * rows, rows), :].reshape(dates * rows, LANES)
                    for s, y in sources
                ],
                axis=1,
            )
            right = jnp.concatenate([root[home, slot + s, y] for s, y in sources], axis=0)
            shocks = jnp.dot(left, right, preferred_element_type=F32)
            pull = pull_ref[pl.ds(factor_block(col, zx), 1), :]
            state = jnp.zeros((rows, LANES), F32)
            for date in range(dates):
                state = pull * state + shocks[date * rows:(date + 1) * rows]
                levels = state.astype(BF16)
                for chunk in range(CHUNKS // HALVES):
                    book[
                        part * (CHUNKS // HALVES) + chunk, place["z"], place["x"], col, place["y"],
                        pl.ds(date * part_rows, part_rows), :,
                    ] = levels[chunk * part_rows:(chunk + 1) * part_rows]

    plans = [part_steps(place, order) for _, _, order in PARTS]

    def view(part, chunk, coords, half):
        (col, cols), (row, rows), _ = PARTS[part]
        if half is not None:
            rows = rows // 2
            row = row + half * rows
        pick = [slice(None) if coords[a] is None else coords[a] for a in "zxy"]
        return book.at[chunk, pick[0], pick[1], pl.ds(col, cols), pick[2], pl.ds(row, rows), :]

    def descriptors(part, step, chunk, kind):
        sends, recvs = plans[part][step]
        for way in range(len(sends)):
            if kind == "send":
                coords, half, target = sends[way]
            else:
                coords, half = recvs[way]
                target = place
            ref = view(part, chunk, coords, half)
            yield remote(
                ref, ref, send_sems.at[chunk, part, step, way], recv_sems.at[chunk, part, step, way],
                trade=trade_index(target),
            )

    def start(chunk):
        for part in range(len(PARTS)):
            for copy in descriptors(part, 0, chunk, "send"):
                copy.start()

    def advance(step, chunk):
        for part in range(len(PARTS)):
            hand_on(
                descriptors(part, step - 1, chunk, "recv"), descriptors(part, step, chunk, "send"),
                plans[part][step][0][0][1] is not None,
            )

    def complete(chunk):
        for part in range(len(PARTS)):
            for copy in descriptors(part, STEPS - 1, chunk, "recv"):
                copy.wait_recv()

    half_chunks = CHUNKS // HALVES

    def both(part, act):
        @pl.loop(part * half_chunks, (part + 1) * half_chunks)
        def _(chunk):
            act(chunk)

    draw_arrived(2, 0)
    make_levels(0)
    both(0, start)
    both(0, functools.partial(advance, 1))
    both(0, functools.partial(advance, 2))
    draw_arrived(2, 1)
    make_levels(1)
    both(1, start)
    advance(3, 0)
    both(1, functools.partial(advance, 1))
    advance(3, 1)
    both(1, functools.partial(advance, 2))

    @pl.loop(0, CHUNKS - 2)
    def _(chunk):
        advance(4, chunk)
        advance(3, chunk + 2)

    def net_copy(late, target):
        first, count = NET_GROUPS[late]
        return remote(
            net_out.at[target, pl.ds(first, count)], net_in.at[me, pl.ds(first, count)],
            net_send_sems.at[late], net_recv_sems.at[late], trade=target,
        )

    def send_nets(late):
        @pl.loop(1, N_TRADE)
        def _(step):
            net_copy(late, (me + step) % N_TRADE).start()

    def await_nets(late):
        first, count = NET_GROUPS[late]
        whole = remote(
            net_out.at[pl.ds(0, N_TRADE - 1), pl.ds(first, count)],
            net_in.at[pl.ds(0, N_TRADE - 1), pl.ds(first, count)],
            net_send_sems.at[late], net_recv_sems.at[late], trade=me,
        )
        whole.wait_send()
        whole.wait_recv()

    def add_nets(chunk):
        total = jnp.zeros((SETS_DEV, NY * ROWS), F32)
        for sender in range(N_TRADE):
            total = total + net_in[sender, chunk].astype(F32)
        net[pl.ds(pl.multiple_of(chunk * SETS_DEV, SETS_DEV), SETS_DEV), :] = jnp.maximum(total, 0.0)

    def compute(chunk):
        net[...] = jnp.zeros_like(net)
        levels = jnp.concatenate(
            [
                book[chunk, owner // NX, owner % NX, col].reshape(NY * ROWS, LANES)
                for col in range(COLS) for owner in range(NZ * NX)[:: 1 - 2 * (col % 2)]
            ],
            axis=1,
        )

        def strip(tile):
            return pl.ds(pl.multiple_of(tile * TILE, TILE), TILE)

        def price(tile, slot):
            prices[slot] = jnp.dot(levels, sens[:, strip(tile)], preferred_element_type=F32)

        def settle(tile, slot):
            at = strip(tile)
            values = weight[:, at] * softplus(prices[slot] + shift_ref[:, at])
            net[...] += lax.dot_general(
                member[:, at], values.astype(BF16), (((1,), (1,)), ((), ())),
                preferred_element_type=F32,
            )

        tiles = positions // TILE
        price(0, 0)

        @pl.loop(0, tiles // 2 - 1)
        def _(pair):
            price(2 * pair + 1, 1)
            settle(2 * pair, 0)
            price(2 * pair + 2, 0)
            settle(2 * pair + 1, 1)

        price(tiles - 1, 1)
        settle(tiles - 2, 0)
        settle(tiles - 1, 1)

        for owner in range(N_TRADE):
            net_out[owner, chunk] = net[owner * SETS_DEV:(owner + 1) * SETS_DEV].astype(BF16)
        net_in[me, chunk] = net_out[me, chunk]

    weight[...] = jnp.where(
        lax.broadcasted_iota(jnp.int32, (1, positions), 1) < live_ref[...],
        principal_ref[...], 0.0,
    )

    @pl.loop(0, positions // TILE)
    def _(tile):
        at = pl.ds(pl.multiple_of(tile * TILE, TILE), TILE)
        labels = lax.broadcasted_iota(jnp.int32, (sets, TILE), 0)
        member[:, at] = (labels == group_ref[:, at]).astype(F32).astype(BF16)

    fetch.wait()

    @pl.loop(0, CHUNKS)
    def _(chunk):
        @pl.when(chunk == CHUNKS - 3)
        def _():
            advance(4, CHUNKS - 2)

        @pl.when(chunk == CHUNKS - 2)
        def _():
            advance(4, CHUNKS - 1)
            send_nets(0)

        complete(chunk)

        @pl.when(chunk == CHUNKS - 1)
        def _():
            send_nets(1)

        compute(chunk)

    send_nets(2)

    for by in range(1, NY):
        draw_copy(by, place["y"]).wait_send()
    for part in range(HALVES):
        for step in range(DRAW_STEPS):
            for copy in draw_ring(step, "send", part):
                copy.wait_send()
    for kind in range(2):
        @pl.when(zx < kinds[kind][1])
        def _(kind=kind):
            @pl.loop(1, NZ * NX)
            def _(step):
                root_copy(kind, (zx + step) % (NZ * NX), zx).wait_send()
    for step in range(3):
        for copy in root_ring(step, "send"):
            copy.wait_send()
    for by in range(NY):
        twin_copy(by, core).wait_send()

    @pl.loop(0, CHUNKS)
    def _(chunk):
        for part in range(len(PARTS)):
            for step in range(STEPS):
                for copy in descriptors(part, step, chunk, "send"):
                    copy.wait_send()

    for late, (first, count) in enumerate(NET_GROUPS):
        await_nets(late)

        @pl.loop(first, first + count)
        def _(chunk):
            add_nets(chunk)

    mean_in[scen] = jnp.zeros(mean_in.shape[1:], F32)
    down = lax.broadcasted_iota(jnp.int32, (SETS_DEV, LANES), 0)
    across = lax.broadcasted_iota(jnp.int32, (SETS_DEV, LANES), 1)
    for date in range(dates):
        strip = jnp.concatenate(
            [
                net[chunk * SETS_DEV:(chunk + 1) * SETS_DEV, y * ROWS + date * part_rows:][:, :part_rows]
                for y in range(NY) for chunk in range(CHUNKS)
            ],
            axis=1,
        )
        out_ref[date] = strip
        sums = jnp.where(down == across, jnp.sum(strip, axis=1, keepdims=True), 0.0)
        mean_in[scen, pl.ds(date, 1), :] = jnp.sum(sums, axis=0, keepdims=True)

    def mean_copy(by, slot):
        return remote(
            mean_in.at[slot], mean_in.at[slot], mean_send.at[by - 1], mean_recv.at[by - 1],
            scen=(scen + by) % scens,
        )

    for by in range(1, scens):
        mean_copy(by, scen).start()

    for by in range(1, scens):
        mean_copy(by, (scen + scens - by) % scens).wait_recv()
        mean_copy(by, scen).wait_send()
    total = jnp.sum(mean_in[...], axis=0) / (scens * NY * span)
    mean_ref[...] = total[:dates, :SETS_DEV]


def exposures(draws, root, sensitivity, pull, shift, principal, group, live):
    dates, scen, _ = draws.shape
    positions = sensitivity.shape[1]
    sets = SETS_DEV * N_TRADE
    span = scen // NY
    vmem = pl.BlockSpec(memory_space=pltpu.VMEM)
    hbm = pl.BlockSpec(memory_space=pl.ANY)
    dma = pltpu.SemaphoreType.DMA
    return pl.pallas_call(
        exposure_kernel,
        out_shape=(
            jax.ShapeDtypeStruct((dates, SETS_DEV, scen), F32),
            jax.ShapeDtypeStruct((dates, SETS_DEV), F32),
        ),
        in_specs=[hbm, hbm, hbm, vmem, vmem, vmem, vmem, vmem],
        out_specs=(vmem, vmem),
        scratch_shapes=[
            pltpu.VMEM((NZ, NX, NY, dates, span, LANES), BF16),
            pltpu.VMEM((2, SLOTS, NY, LANES, LANES), BF16),
            pltpu.VMEM((CHUNKS, NZ, NX, COLS, NY, ROWS, LANES), BF16),
            pltpu.VMEM(sensitivity.shape, BF16),
            pltpu.VMEM((sets, positions), BF16),
            pltpu.VMEM((1, positions), F32),
            pltpu.VMEM((sets, NY * ROWS), F32),
            pltpu.VMEM((2, NY * ROWS, TILE), F32),
            pltpu.VMEM((N_TRADE, CHUNKS, SETS_DEV, NY * ROWS), BF16),
            pltpu.VMEM((N_TRADE, CHUNKS, SETS_DEV, NY * ROWS), BF16),
            pltpu.VMEM((lax.axis_size("scen"), 8, LANES), F32),
            dma((NY - 1,)), dma((NY - 1,)),
            dma((HALVES, dates, DRAW_STEPS, 2)), dma((HALVES, dates, DRAW_STEPS, 2)),
            dma((2, NZ * NX)), dma((2, NZ * NX)),
            dma((3, 2)), dma((3, 2)), dma((NY,)), dma((NY,)),
            dma((CHUNKS, len(PARTS), STEPS, 2)), dma((CHUNKS, len(PARTS), STEPS, 2)),
            dma((3,)), dma, dma((len(NET_GROUPS),)), dma((len(NET_GROUPS),)),
            dma((lax.axis_size("scen") - 1,)), dma((lax.axis_size("scen") - 1,)),
        ],
        compiler_params=pltpu.CompilerParams(
            collective_id=1, has_side_effects=True, vmem_limit_bytes=58 * 2**20
        ),
        cost_estimate=pl.CostEstimate(
            flops=2 * 1024 * positions * (4096 + sets), bytes_accessed=17 << 20, transcendentals=0
        ),
        name="exposures",
    )(
        draws, root, sensitivity, pull.reshape(-1, LANES), shift.reshape(1, -1),
        principal.reshape(1, -1), group.reshape(1, -1), live.reshape(1, 1),
    )


def on_device(
    normal_draws, covariance_root, mean_pullback, sensitivity_tensor,
    moneyness_shift, signed_principal, deal_agreement_group, active_position_number,
):
    exposure, mean = exposures(
        normal_draws, covariance_root, sensitivity_tensor, mean_pullback, moneyness_shift,
        signed_principal, deal_agreement_group, active_position_number,
    )
    return exposure.transpose(0, 2, 1), mean


def solution(mesh):
    in_specs = (
        P(None, "scen", "trade"), P("trade", None), P(), P(None, "trade"),
        P("trade"), P("trade"), P("trade"), P("trade"),
    )
    out_specs = (P(None, "scen", "trade"), P(None, "trade"))
    return jax.shard_map(
        on_device, mesh=mesh, in_specs=in_specs, out_specs=out_specs, check_vma=False
    )
```

```python
import functools
import jax
import jax.numpy as jnp
from jax import lax
from jax.experimental import pallas as pl
from jax.experimental.pallas import tpu as pltpu
from jax.sharding import PartitionSpec as P

F32, BF16 = jnp.float32, jnp.bfloat16
SETS_DEV = 16
NZ, NX, NY = 2, 4, 4
N_TRADE = NZ * NX * NY
CHUNKS = 4
COLS = 4
ROWS = 64
LANES = 128
TILE = 512
HALVES = 2
PARTS = (
    ((0, 3), (0, 32), ("z", "y", "x")),
    ((0, 3), (32, 32), ("z", "x", "y")),
    ((3, 1), (0, 32), ("x", "y", "z")),
    ((3, 1), (32, 32), ("y", "x", "z")),
)
STEPS = 5
DRAW_ORDERS = (("z", "x"), ("x", "z"))
DRAW_STEPS = 3
SLOTS = 10
NET_GROUPS = ((0, CHUNKS - 1), (CHUNKS - 1, 1))


def trade_place():
    me = lax.axis_index("trade")
    return {"z": me // (NX * NY), "x": (me // NY) % NX, "y": me % NY}


def trade_index(place):
    return (place["z"] * NX + place["x"]) * NY + place["y"]


def moved(place, axis, by):
    size = {"z": NZ, "x": NX, "y": NY}[axis]
    return dict(place, **{axis: (place[axis] + by) % size})


def part_steps(place, order):
    have = dict(place)
    steps = []
    for axis in order:
        if axis == "z":
            steps.append(
                (
                    [(dict(have), None, moved(place, "z", 1))],
                    [(dict(have, z=1 - place["z"]), None)],
                )
            )
        else:
            right, left = moved(place, axis, 1), moved(place, axis, 3)
            far = moved(place, axis, 2)
            at = lambda where: dict(have, **{axis: where[axis]})
            steps.append(
                (
                    [(at(place), None, right), (at(place), None, left)],
                    [(at(left), None), (at(right), None)],
                )
            )
            steps.append(
                (
                    [(at(left), 0, right), (at(right), 1, left)],
                    [(at(far), 0), (at(far), 1)],
                )
            )
        have[axis] = None
    return steps


def hand_on(arrivals, sends, pairwise):
    arrivals, sends = list(arrivals), list(sends)
    if pairwise:
        for arrival, send in zip(arrivals, sends):
            arrival.wait_recv()
            send.start()
    else:
        for arrival in arrivals:
            arrival.wait_recv()
        for send in sends:
            send.start()


def softplus(a):
    return jnp.maximum(a, 0.0) + jnp.log(1.0 + jnp.exp(-jnp.abs(a)))


def factor_block(col, owner):
    return 8 * col + (owner if col % 2 == 0 else 7 - owner)


def column_home(col):
    return {3: (0, 0), 0: (0, 8), 2: (1, 0), 1: (1, 6)}[col]


def exposure_kernel(
    draws_hbm, root_hbm, sens_hbm, pull_ref, shift_ref, principal_ref, group_ref, live_ref,
    out_ref, mean_ref,
    draws, root, book, sens, member, weight, net, prices, net_out, net_in, mean_in,
    draw_send, draw_recv, draw_ring_send, draw_ring_recv,
    root_send, root_recv, root_ring_send, root_ring_recv, twin_send, twin_recv,
    send_sems, recv_sems, own_sems, sens_sem, net_send_sems, net_recv_sems,
    mean_send, mean_recv,
):
    place = trade_place()
    me = trade_index(place)
    zx = place["z"] * NX + place["x"]
    scen = lax.axis_index("scen")
    scens = lax.axis_size("scen")
    core = scen % 2
    twin = scen + 1 - 2 * core
    positions = sens.shape[1]
    sets = member.shape[0]
    span = draws_hbm.shape[1] // NY

    def remote(src, dst, send, recv, **target):
        return pltpu.make_async_remote_copy(
            src_ref=src, dst_ref=dst, send_sem=send, recv_sem=recv,
            device_id=target, device_id_type=pl.DeviceIdType.MESH,
        )

    barrier = pltpu.get_barrier_semaphore()

    for step in range(1, N_TRADE):
        pl.semaphore_signal(
            barrier, inc=1, device_id={"trade": lax.rem(me + step, N_TRADE)},
            device_id_type=pl.DeviceIdType.MESH,
        )

    @pl.loop(1, scens)
    def _(step):
        pl.semaphore_signal(
            barrier, inc=1, device_id={"scen": (scen + step) % scens},
            device_id_type=pl.DeviceIdType.MESH,
        )

    pl.semaphore_wait(barrier, N_TRADE - 1 + scens - 1)

    def draw_rows(y):
        return draws_hbm.at[:, pl.ds(y * span, span), :]

    def draw_copy(by, source):
        return remote(
            draw_rows((place["y"] + by) % NY), draws.at[place["z"], place["x"], source],
            draw_send.at[by - 1], draw_recv.at[by - 1],
            trade=trade_index(moved(place, "y", by)),
        )

    own_draws = pltpu.make_async_copy(
        draw_rows(place["y"]), draws.at[place["z"], place["x"], place["y"]], own_sems.at[0]
    )
    own_draws.start()
    for by in range(1, NY):
        draw_copy(by, place["y"]).start()

    high_count, low_count = 8 - 2 * core, 2 + 2 * core
    kinds = ((3 - core, high_count, 0), (core, low_count, high_count))

    def root_block(kind, owner):
        col = kinds[kind][0]
        block = 8 * col + jnp.where(col % 2 == 0, owner, 7 - owner)
        return root_hbm.at[:, pl.ds(pl.multiple_of(block * LANES, LANES), LANES)]

    def root_slot(kind, source):
        return root.at[core, kinds[kind][2] + source, place["y"]]

    def root_copy(kind, owner, source):
        return remote(
            root_block(kind, owner), root_slot(kind, source),
            root_send.at[kind, owner], root_recv.at[kind, source],
            trade=owner * NY + place["y"],
        )

    def own_root(kind):
        return pltpu.make_async_copy(root_block(kind, zx), root_slot(kind, zx), own_sems.at[1 + kind])

    for kind in range(2):
        @pl.when(zx < kinds[kind][1])
        def _(kind=kind):
            own_root(kind).start()

            @pl.loop(1, NZ * NX)
            def _(step):
                root_copy(kind, (zx + step) % (NZ * NX), zx).start()

    fetch = pltpu.make_async_copy(sens_hbm, sens, sens_sem)
    fetch.start()

    draw_plans = [part_steps(place, order) for order in DRAW_ORDERS]

    def draw_ring(step, kind, part, only=None):
        for date, plan in reversed(list(enumerate(draw_plans))):
            if only is not None and date != only:
                continue
            sends, recvs = plan[step]
            for way in range(len(sends)):
                coords, half = (sends if kind == "send" else recvs)[way][:2]
                target = sends[way][2]
                rows = span // HALVES
                row = part * rows
                if half is not None:
                    rows = rows // 2
                    row = row + half * rows
                pick = [slice(None) if coords[a] is None else coords[a] for a in "zx"]
                ref = draws.at[pick[0], pick[1], :, date, pl.ds(row, rows), :]
                yield remote(
                    ref, ref, draw_ring_send.at[part, date, step, way],
                    draw_ring_recv.at[part, date, step, way],
                    trade=trade_index(target),
                )

    def root_ring(step, kind):
        y = place["y"]
        right, left = moved(place, "y", 1), moved(place, "y", 3)
        far = (y + 2) % NY
        half = SLOTS // 2
        if step < 2:
            at = {"send": (y, y), "recv": (left["y"], right["y"])}[kind]
        else:
            at = {"send": (left["y"], right["y"]), "recv": (far, far)}[kind]
        refs = [
            root.at[core, pl.ds(half * (way if step != 1 else 1 - way), half), a]
            for way, a in enumerate(at)
        ]
        for way, target in enumerate((right, left)):
            yield remote(
                refs[way], refs[way], root_ring_send.at[step, way], root_ring_recv.at[step, way],
                trade=trade_index(target),
            )

    def twin_copy(by, from_core):
        ref = root.at[from_core, :, (place["y"] + by) % NY]
        return remote(ref, ref, twin_send.at[by], twin_recv.at[by], scen=twin)

    own_draws.wait()
    for by in range(1, NY):
        draw_copy(by, (place["y"] + NY - by) % NY).wait_recv()
    def draw_start(step, part):
        for copy in draw_ring(step, "send", part):
            copy.start()

    def draw_advance(step, part):
        for date, plan in reversed(list(enumerate(draw_plans))):
            hand_on(
                draw_ring(step - 1, "recv", part, date), draw_ring(step, "send", part, date),
                plan[step][0][0][1] is not None,
            )

    def draw_arrived(step, part):
        for copy in draw_ring(step, "recv", part):
            copy.wait_recv()

    for part in range(HALVES):
        draw_start(0, part)

    for kind in range(2):
        @pl.when(zx < kinds[kind][1])
        def _(kind=kind):
            own_root(kind).wait()

        @pl.loop(0, NZ * NX)
        def _(source, kind=kind):
            @pl.when(jnp.logical_and(source < kinds[kind][1], source != zx))
            def _():
                root_copy(kind, zx, source).wait_recv()
    for step in range(2):
        for copy in root_ring(step, "send"):
            copy.start()
    twin_copy(0, core).start()

    for part in range(HALVES):
        draw_advance(1, part)

    hand_on(root_ring(0, "recv"), root_ring(2, "send"), True)
    for copy in root_ring(1, "recv"):
        copy.wait_recv()
    twin_copy(1, core).start()
    twin_copy(3, core).start()

    for part in range(HALVES):
        draw_advance(2, part)

    for copy in root_ring(2, "recv"):
        copy.wait_recv()
    twin_copy(2, core).start()

    for by in range(NY):
        twin_copy(by, 1 - core).wait_recv()

    dates = draws.shape[3]
    part_rows = span // CHUNKS

    def make_levels(part):
        rows = span // HALVES
        for col in range(COLS):
            home, slot = column_home(col)
            sources = [(s, y) for s in range(2 * (col + 1)) for y in range(NY)]
            left = jnp.concatenate(
                [
                    draws[s // NX, s % NX, y, :, pl.ds(part * rows, rows), :].reshape(dates * rows, LANES)
                    for s, y in sources
                ],
                axis=1,
            )
            right = jnp.concatenate([root[home, slot + s, y] for s, y in sources], axis=0)
            shocks = jnp.dot(left, right, preferred_element_type=F32)
            pull = pull_ref[pl.ds(factor_block(col, zx), 1), :]
            state = jnp.zeros((rows, LANES), F32)
            for date in range(dates):
                state = pull * state + shocks[date * rows:(date + 1) * rows]
                levels = state.astype(BF16)
                for chunk in range(CHUNKS // HALVES):
                    book[
                        part * (CHUNKS // HALVES) + chunk, place["z"], place["x"], col, place["y"],
                        pl.ds(date * part_rows, part_rows), :,
                    ] = levels[chunk * part_rows:(chunk + 1) * part_rows]

    plans = [part_steps(place, order) for _, _, order in PARTS]

    def view(part, chunk, coords, half):
        (col, cols), (row, rows), _ = PARTS[part]
        if half is not None:
            rows = rows // 2
            row = row + half * rows
        pick = [slice(None) if coords[a] is None else coords[a] for a in "zxy"]
        return book.at[chunk, pick[0], pick[1], pl.ds(col, cols), pick[2], pl.ds(row, rows), :]

    def descriptors(part, step, chunk, kind):
        sends, recvs = plans[part][step]
        for way in range(len(sends)):
            if kind == "send":
                coords, half, target = sends[way]
            else:
                coords, half = recvs[way]
                target = place
            ref = view(part, chunk, coords, half)
            yield remote(
                ref, ref, send_sems.at[chunk, part, step, way], recv_sems.at[chunk, part, step, way],
                trade=trade_index(target),
            )

    def start(chunk):
        for part in range(len(PARTS)):
            for copy in descriptors(part, 0, chunk, "send"):
                copy.start()

    def advance(step, chunk):
        for part in range(len(PARTS)):
            hand_on(
                descriptors(part, step - 1, chunk, "recv"), descriptors(part, step, chunk, "send"),
                plans[part][step][0][0][1] is not None,
            )

    def complete(chunk):
        for part in range(len(PARTS)):
            for copy in descriptors(part, STEPS - 1, chunk, "recv"):
                copy.wait_recv()

    half_chunks = CHUNKS // HALVES

    def both(part, act):
        @pl.loop(part * half_chunks, (part + 1) * half_chunks)
        def _(chunk):
            act(chunk)

    draw_arrived(2, 0)
    make_levels(0)
    both(0, start)
    both(0, functools.partial(advance, 1))
    draw_arrived(2, 1)
    make_levels(1)
    both(1, start)
    both(0, functools.partial(advance, 2))
    both(1, functools.partial(advance, 1))
    advance(3, 0)
    advance(2, 2)
    advance(3, 1)
    advance(2, 3)

    @pl.loop(0, CHUNKS - 2)
    def _(chunk):
        advance(4, chunk)
        advance(3, chunk + 2)

    def net_copy(late, target):
        first, count = NET_GROUPS[late]
        return remote(
            net_out.at[target, pl.ds(first, count)], net_in.at[me, pl.ds(first, count)],
            net_send_sems.at[late], net_recv_sems.at[late], trade=target,
        )

    def send_nets(late):
        for step in range(1, N_TRADE):
            net_copy(late, lax.rem(me + step, N_TRADE)).start()

    def await_nets(late):
        first, count = NET_GROUPS[late]
        whole = remote(
            net_out.at[pl.ds(0, N_TRADE - 1), pl.ds(first, count)],
            net_in.at[pl.ds(0, N_TRADE - 1), pl.ds(first, count)],
            net_send_sems.at[late], net_recv_sems.at[late], trade=me,
        )
        whole.wait_send()
        whole.wait_recv()

    def add_nets(chunk):
        total = jnp.zeros((SETS_DEV, NY * ROWS), F32)
        for sender in range(N_TRADE):
            total = total + net_in[sender, chunk].astype(F32)
        net[pl.ds(pl.multiple_of(chunk * SETS_DEV, SETS_DEV), SETS_DEV), :] = jnp.maximum(total, 0.0)

    def compute(chunk):
        net[...] = jnp.zeros_like(net)
        levels = jnp.concatenate(
            [
                book[chunk, owner // NX, owner % NX, col].reshape(NY * ROWS, LANES)
                for col in range(COLS) for owner in range(NZ * NX)[:: 1 - 2 * (col % 2)]
            ],
            axis=1,
        )

        def strip(tile):
            return pl.ds(pl.multiple_of(tile * TILE, TILE), TILE)

        def price(tile, slot):
            prices[slot] = jnp.dot(levels, sens[:, strip(tile)], preferred_element_type=F32)

        def settle(tile, slot):
            at = strip(tile)
            values = weight[:, at] * softplus(prices[slot] + shift_ref[:, at])
            net[...] += lax.dot_general(
                member[:, at], values.astype(BF16), (((1,), (1,)), ((), ())),
                preferred_element_type=F32,
            )

        tiles = positions // TILE
        price(0, 0)

        @pl.loop(0, tiles // 2 - 1)
        def _(pair):
            price(2 * pair + 1, 1)
            settle(2 * pair, 0)

            @pl.when(chunk < CHUNKS - 2)
            def _():
                advance(4, chunk + 2)

            price(2 * pair + 2, 0)
            settle(2 * pair + 1, 1)

        price(tiles - 1, 1)
        settle(tiles - 2, 0)
        settle(tiles - 1, 1)

        for owner in range(N_TRADE):
            net_out[owner, chunk] = net[owner * SETS_DEV:(owner + 1) * SETS_DEV].astype(BF16)
        net_in[me, chunk] = net_out[me, chunk]

    weight[...] = jnp.where(
        lax.broadcasted_iota(jnp.int32, (1, positions), 1) < live_ref[...],
        principal_ref[...], 0.0,
    )

    @pl.loop(0, positions // TILE)
    def _(tile):
        at = pl.ds(pl.multiple_of(tile * TILE, TILE), TILE)
        labels = lax.broadcasted_iota(jnp.int32, (sets, TILE), 0)
        member[:, at] = (labels == group_ref[:, at]).astype(F32).astype(BF16)

    fetch.wait()

    @pl.loop(0, CHUNKS)
    def _(chunk):
        complete(chunk)

        @pl.when(chunk == CHUNKS - 1)
        def _():
            send_nets(0)

        compute(chunk)

    send_nets(1)

    for by in range(1, NY):
        draw_copy(by, place["y"]).wait_send()
    for part in range(HALVES):
        for step in range(DRAW_STEPS):
            for copy in draw_ring(step, "send", part):
                copy.wait_send()
    for kind in range(2):
        @pl.when(zx < kinds[kind][1])
        def _(kind=kind):
            @pl.loop(1, NZ * NX)
            def _(step):
                root_copy(kind, (zx + step) % (NZ * NX), zx).wait_send()
    for step in range(3):
        for copy in root_ring(step, "send"):
            copy.wait_send()
    for by in range(NY):
        twin_copy(by, core).wait_send()

    @pl.loop(0, CHUNKS)
    def _(chunk):
        for part in range(len(PARTS)):
            for step in range(STEPS):
                for copy in descriptors(part, step, chunk, "send"):
                    copy.wait_send()

    for late, (first, count) in enumerate(NET_GROUPS):
        await_nets(late)

        @pl.loop(first, first + count)
        def _(chunk):
            add_nets(chunk)

    mean_in[scen] = jnp.zeros(mean_in.shape[1:], F32)
    down = lax.broadcasted_iota(jnp.int32, (SETS_DEV, LANES), 0)
    across = lax.broadcasted_iota(jnp.int32, (SETS_DEV, LANES), 1)
    for date in range(dates):
        strip = jnp.concatenate(
            [
                net[chunk * SETS_DEV:(chunk + 1) * SETS_DEV, y * ROWS + date * part_rows:][:, :part_rows]
                for y in range(NY) for chunk in range(CHUNKS)
            ],
            axis=1,
        )
        out_ref[date] = strip
        sums = jnp.where(down == across, jnp.sum(strip, axis=1, keepdims=True), 0.0)
        mean_in[scen, pl.ds(date, 1), :] = jnp.sum(sums, axis=0, keepdims=True)

    def mean_copy(by, slot):
        return remote(
            mean_in.at[slot], mean_in.at[slot], mean_send.at[by - 1], mean_recv.at[by - 1],
            scen=(scen + by) % scens,
        )

    for by in range(1, scens):
        mean_copy(by, scen).start()

    for by in range(1, scens):
        mean_copy(by, (scen + scens - by) % scens).wait_recv()
        mean_copy(by, scen).wait_send()
    total = jnp.sum(mean_in[...], axis=0) / (scens * NY * span)
    mean_ref[...] = total[:dates, :SETS_DEV]


def exposures(draws, root, sensitivity, pull, shift, principal, group, live):
    dates, scen, _ = draws.shape
    positions = sensitivity.shape[1]
    sets = SETS_DEV * N_TRADE
    span = scen // NY
    vmem = pl.BlockSpec(memory_space=pltpu.VMEM)
    hbm = pl.BlockSpec(memory_space=pl.ANY)
    dma = pltpu.SemaphoreType.DMA
    return pl.pallas_call(
        exposure_kernel,
        out_shape=(
            jax.ShapeDtypeStruct((dates, SETS_DEV, scen), F32),
            jax.ShapeDtypeStruct((dates, SETS_DEV), F32),
        ),
        in_specs=[hbm, hbm, hbm, vmem, vmem, vmem, vmem, vmem],
        out_specs=(vmem, vmem),
        scratch_shapes=[
            pltpu.VMEM((NZ, NX, NY, dates, span, LANES), BF16),
            pltpu.VMEM((2, SLOTS, NY, LANES, LANES), BF16),
            pltpu.VMEM((CHUNKS, NZ, NX, COLS, NY, ROWS, LANES), BF16),
            pltpu.VMEM(sensitivity.shape, BF16),
            pltpu.VMEM((sets, positions), BF16),
            pltpu.VMEM((1, positions), F32),
            pltpu.VMEM((sets, NY * ROWS), F32),
            pltpu.VMEM((2, NY * ROWS, TILE), F32),
            pltpu.VMEM((N_TRADE, CHUNKS, SETS_DEV, NY * ROWS), BF16),
            pltpu.VMEM((N_TRADE, CHUNKS, SETS_DEV, NY * ROWS), BF16),
            pltpu.VMEM((lax.axis_size("scen"), 8, LANES), F32),
            dma((NY - 1,)), dma((NY - 1,)),
            dma((HALVES, dates, DRAW_STEPS, 2)), dma((HALVES, dates, DRAW_STEPS, 2)),
            dma((2, NZ * NX)), dma((2, NZ * NX)),
            dma((3, 2)), dma((3, 2)), dma((NY,)), dma((NY,)),
            dma((CHUNKS, len(PARTS), STEPS, 2)), dma((CHUNKS, len(PARTS), STEPS, 2)),
            dma((3,)), dma, dma((len(NET_GROUPS),)), dma((len(NET_GROUPS),)),
            dma((lax.axis_size("scen") - 1,)), dma((lax.axis_size("scen") - 1,)),
        ],
        compiler_params=pltpu.CompilerParams(
            collective_id=1, has_side_effects=True, vmem_limit_bytes=58 * 2**20
        ),
        cost_estimate=pl.CostEstimate(
            flops=2 * 1024 * positions * (4096 + sets), bytes_accessed=17 << 20, transcendentals=0
        ),
        name="exposures",
    )(
        draws, root, sensitivity, pull.reshape(-1, LANES), shift.reshape(1, -1),
        principal.reshape(1, -1), group.reshape(1, -1), live.reshape(1, 1),
    )


def on_device(
    normal_draws, covariance_root, mean_pullback, sensitivity_tensor,
    moneyness_shift, signed_principal, deal_agreement_group, active_position_number,
):
    exposure, mean = exposures(
        normal_draws, covariance_root, sensitivity_tensor, mean_pullback, moneyness_shift,
        signed_principal, deal_agreement_group, active_position_number,
    )
    return exposure.transpose(0, 2, 1), mean


def solution(mesh):
    in_specs = (
        P(None, "scen", "trade"), P("trade", None), P(), P(None, "trade"),
        P("trade"), P("trade"), P("trade"), P("trade"),
    )
    out_specs = (P(None, "scen", "trade"), P(None, "trade"))
    return jax.shard_map(
        on_device, mesh=mesh, in_specs=in_specs, out_specs=out_specs, check_vma=False
    )
```

```python
import functools
import jax
import jax.numpy as jnp
from jax import lax
from jax.experimental import pallas as pl
from jax.experimental.pallas import tpu as pltpu
from jax.sharding import PartitionSpec as P

F32, BF16 = jnp.float32, jnp.bfloat16
SETS_DEV = 16
NZ, NX, NY = 2, 4, 4
N_TRADE = NZ * NX * NY
CHUNKS = 4
COLS = 4
ROWS = 64
LANES = 128
TILE = 512
HALVES = 2
PARTS = (
    ((0, 3), (0, 32), ("z", "y", "x")),
    ((0, 3), (32, 32), ("z", "x", "y")),
    ((3, 1), (0, 32), ("x", "y", "z")),
    ((3, 1), (32, 32), ("y", "x", "z")),
)
STEPS = 5
DRAW_ORDERS = (("z", "x"), ("x", "z"))
DRAW_STEPS = 3
SLOTS = 10
NET_GROUPS = ((0, CHUNKS - 1), (CHUNKS - 1, 1))


def trade_place():
    me = lax.axis_index("trade")
    return {"z": me // (NX * NY), "x": (me // NY) % NX, "y": me % NY}


def trade_index(place):
    return (place["z"] * NX + place["x"]) * NY + place["y"]


def moved(place, axis, by):
    size = {"z": NZ, "x": NX, "y": NY}[axis]
    return dict(place, **{axis: (place[axis] + by) % size})


def part_steps(place, order):
    have = dict(place)
    steps = []
    for axis in order:
        if axis == "z":
            steps.append(
                (
                    [(dict(have), None, moved(place, "z", 1))],
                    [(dict(have, z=1 - place["z"]), None)],
                )
            )
        else:
            right, left = moved(place, axis, 1), moved(place, axis, 3)
            far = moved(place, axis, 2)
            at = lambda where: dict(have, **{axis: where[axis]})
            steps.append(
                (
                    [(at(place), None, right), (at(place), None, left)],
                    [(at(left), None), (at(right), None)],
                )
            )
            steps.append(
                (
                    [(at(left), 0, right), (at(right), 1, left)],
                    [(at(far), 0), (at(far), 1)],
                )
            )
        have[axis] = None
    return steps


def hand_on(arrivals, sends, pairwise):
    arrivals, sends = list(arrivals), list(sends)
    if pairwise:
        for arrival, send in zip(arrivals, sends):
            arrival.wait_recv()
            send.start()
    else:
        for arrival in arrivals:
            arrival.wait_recv()
        for send in sends:
            send.start()


def softplus(a):
    return jnp.maximum(a, 0.0) + jnp.log(1.0 + jnp.exp(-jnp.abs(a)))


def factor_block(col, owner):
    return 8 * col + (owner if col % 2 == 0 else 7 - owner)


def column_home(col):
    return {3: (0, 0), 0: (0, 8), 2: (1, 0), 1: (1, 6)}[col]


def exposure_kernel(
    draws_hbm, root_hbm, sens_hbm, pull_ref, shift_ref, principal_ref, group_ref, live_ref,
    out_ref, mean_ref,
    draws, root, book, sens, member, weight, net, prices, net_out, net_in, mean_in,
    draw_send, draw_recv, draw_ring_send, draw_ring_recv,
    root_send, root_recv, root_ring_send, root_ring_recv, twin_send, twin_recv,
    send_sems, recv_sems, own_sems, sens_sem, net_send_sems, net_recv_sems,
    mean_send, mean_recv,
):
    place = trade_place()
    me = trade_index(place)
    zx = place["z"] * NX + place["x"]
    scen = lax.axis_index("scen")
    scens = lax.axis_size("scen")
    core = scen % 2
    twin = scen + 1 - 2 * core
    positions = sens.shape[1]
    sets = member.shape[0]
    span = draws_hbm.shape[1] // NY

    def remote(src, dst, send, recv, **target):
        return pltpu.make_async_remote_copy(
            src_ref=src, dst_ref=dst, send_sem=send, recv_sem=recv,
            device_id=target, device_id_type=pl.DeviceIdType.MESH,
        )

    barrier = pltpu.get_barrier_semaphore()

    greeted = [trade_index(moved(place, "y", by)) for by in range(1, NY)]
    greeted += [lax.rem(me + step * NY, N_TRADE) for step in range(1, NZ * NX)]
    for target in greeted:
        pl.semaphore_signal(
            barrier, inc=1, device_id={"trade": target}, device_id_type=pl.DeviceIdType.MESH,
        )

    @pl.loop(1, scens)
    def _(step):
        pl.semaphore_signal(
            barrier, inc=1, device_id={"scen": (scen + step) % scens},
            device_id_type=pl.DeviceIdType.MESH,
        )

    pl.semaphore_wait(barrier, len(greeted) + scens - 1)

    def draw_rows(y):
        return draws_hbm.at[:, pl.ds(y * span, span), :]

    def draw_copy(by, source):
        return remote(
            draw_rows((place["y"] + by) % NY), draws.at[place["z"], place["x"], source],
            draw_send.at[by - 1], draw_recv.at[by - 1],
            trade=trade_index(moved(place, "y", by)),
        )

    own_draws = pltpu.make_async_copy(
        draw_rows(place["y"]), draws.at[place["z"], place["x"], place["y"]], own_sems.at[0]
    )
    own_draws.start()
    for by in range(1, NY):
        draw_copy(by, place["y"]).start()

    high_count, low_count = 8 - 2 * core, 2 + 2 * core
    kinds = ((3 - core, high_count, 0), (core, low_count, high_count))

    def root_block(kind, owner):
        col = kinds[kind][0]
        block = 8 * col + jnp.where(col % 2 == 0, owner, 7 - owner)
        return root_hbm.at[:, pl.ds(pl.multiple_of(block * LANES, LANES), LANES)]

    def root_slot(kind, source):
        return root.at[core, kinds[kind][2] + source, place["y"]]

    def root_copy(kind, owner, source):
        return remote(
            root_block(kind, owner), root_slot(kind, source),
            root_send.at[kind, owner], root_recv.at[kind, source],
            trade=owner * NY + place["y"],
        )

    def own_root(kind):
        return pltpu.make_async_copy(root_block(kind, zx), root_slot(kind, zx), own_sems.at[1 + kind])

    for kind in range(2):
        @pl.when(zx < kinds[kind][1])
        def _(kind=kind):
            own_root(kind).start()

            @pl.loop(1, NZ * NX)
            def _(step):
                root_copy(kind, (zx + step) % (NZ * NX), zx).start()

    fetch = pltpu.make_async_copy(sens_hbm, sens, sens_sem)
    fetch.start()

    draw_plans = [part_steps(place, order) for order in DRAW_ORDERS]

    def draw_ring(step, kind, part, only=None):
        for date, plan in reversed(list(enumerate(draw_plans))):
            if only is not None and date != only:
                continue
            sends, recvs = plan[step]
            for way in range(len(sends)):
                coords, half = (sends if kind == "send" else recvs)[way][:2]
                target = sends[way][2]
                rows = span // HALVES
                row = part * rows
                if half is not None:
                    rows = rows // 2
                    row = row + half * rows
                pick = [slice(None) if coords[a] is None else coords[a] for a in "zx"]
                ref = draws.at[pick[0], pick[1], :, date, pl.ds(row, rows), :]
                yield remote(
                    ref, ref, draw_ring_send.at[part, date, step, way],
                    draw_ring_recv.at[part, date, step, way],
                    trade=trade_index(target),
                )

    def root_ring(step, kind):
        y = place["y"]
        right, left = moved(place, "y", 1), moved(place, "y", 3)
        far = (y + 2) % NY
        half = SLOTS // 2
        if step < 2:
            at = {"send": (y, y), "recv": (left["y"], right["y"])}[kind]
        else:
            at = {"send": (left["y"], right["y"]), "recv": (far, far)}[kind]
        refs = [
            root.at[core, pl.ds(half * (way if step != 1 else 1 - way), half), a]
            for way, a in enumerate(at)
        ]
        for way, target in enumerate((right, left)):
            yield remote(
                refs[way], refs[way], root_ring_send.at[step, way], root_ring_recv.at[step, way],
                trade=trade_index(target),
            )

    def twin_copy(by, from_core):
        ref = root.at[from_core, :, (place["y"] + by) % NY]
        return remote(ref, ref, twin_send.at[by], twin_recv.at[by], scen=twin)

    own_draws.wait()
    for by in range(1, NY):
        draw_copy(by, (place["y"] + NY - by) % NY).wait_recv()
    def draw_start(step, part):
        for copy in draw_ring(step, "send", part):
            copy.start()

    def draw_advance(step, part):
        for date, plan in reversed(list(enumerate(draw_plans))):
            hand_on(
                draw_ring(step - 1, "recv", part, date), draw_ring(step, "send", part, date),
                plan[step][0][0][1] is not None,
            )

    def draw_arrived(step, part):
        for copy in draw_ring(step, "recv", part):
            copy.wait_recv()

    for part in range(HALVES):
        draw_start(0, part)

    for kind in range(2):
        @pl.when(zx < kinds[kind][1])
        def _(kind=kind):
            own_root(kind).wait()

        @pl.loop(0, NZ * NX)
        def _(source, kind=kind):
            @pl.when(jnp.logical_and(source < kinds[kind][1], source != zx))
            def _():
                root_copy(kind, zx, source).wait_recv()
    for step in range(2):
        for copy in root_ring(step, "send"):
            copy.start()
    twin_copy(0, core).start()

    for part in range(HALVES):
        draw_advance(1, part)

    hand_on(root_ring(0, "recv"), root_ring(2, "send"), True)
    for copy in root_ring(1, "recv"):
        copy.wait_recv()
    twin_copy(1, core).start()
    twin_copy(3, core).start()

    for part in range(HALVES):
        draw_advance(2, part)

    for copy in root_ring(2, "recv"):
        copy.wait_recv()
    twin_copy(2, core).start()

    for by in range(NY):
        twin_copy(by, 1 - core).wait_recv()

    dates = draws.shape[3]
    part_rows = span // CHUNKS

    def make_levels(part):
        rows = span // HALVES
        for col in range(COLS):
            home, slot = column_home(col)
            sources = [(s, y) for s in range(2 * (col + 1)) for y in range(NY)]
            left = jnp.concatenate(
                [
                    draws[s // NX, s % NX, y, :, pl.ds(part * rows, rows), :].reshape(dates * rows, LANES)
                    for s, y in sources
                ],
                axis=1,
            )
            right = jnp.concatenate([root[home, slot + s, y] for s, y in sources], axis=0)
            shocks = jnp.dot(left, right, preferred_element_type=F32)
            pull = pull_ref[pl.ds(factor_block(col, zx), 1), :]
            state = jnp.zeros((rows, LANES), F32)
            for date in range(dates):
                state = pull * state + shocks[date * rows:(date + 1) * rows]
                levels = state.astype(BF16)
                for chunk in range(CHUNKS // HALVES):
                    book[
                        part * (CHUNKS // HALVES) + chunk, place["z"], place["x"], col, place["y"],
                        pl.ds(date * part_rows, part_rows), :,
                    ] = levels[chunk * part_rows:(chunk + 1) * part_rows]

    plans = [part_steps(place, order) for _, _, order in PARTS]

    def view(part, chunk, coords, half):
        (col, cols), (row, rows), _ = PARTS[part]
        if half is not None:
            rows = rows // 2
            row = row + half * rows
        pick = [slice(None) if coords[a] is None else coords[a] for a in "zxy"]
        return book.at[chunk, pick[0], pick[1], pl.ds(col, cols), pick[2], pl.ds(row, rows), :]

    def descriptors(part, step, chunk, kind):
        sends, recvs = plans[part][step]
        for way in range(len(sends)):
            if kind == "send":
                coords, half, target = sends[way]
            else:
                coords, half = recvs[way]
                target = place
            ref = view(part, chunk, coords, half)
            yield remote(
                ref, ref, send_sems.at[chunk, part, step, way], recv_sems.at[chunk, part, step, way],
                trade=trade_index(target),
            )

    def start(chunk):
        for part in range(len(PARTS)):
            for copy in descriptors(part, 0, chunk, "send"):
                copy.start()

    def advance(step, chunk):
        for part in range(len(PARTS)):
            hand_on(
                descriptors(part, step - 1, chunk, "recv"), descriptors(part, step, chunk, "send"),
                plans[part][step][0][0][1] is not None,
            )

    def complete(chunk):
        for part in range(len(PARTS)):
            for copy in descriptors(part, STEPS - 1, chunk, "recv"):
                copy.wait_recv()

    half_chunks = CHUNKS // HALVES

    def both(part, act):
        @pl.loop(part * half_chunks, (part + 1) * half_chunks)
        def _(chunk):
            act(chunk)

    draw_arrived(2, 0)
    make_levels(0)
    both(0, start)
    both(0, functools.partial(advance, 1))
    draw_arrived(2, 1)
    make_levels(1)
    both(1, start)
    both(0, functools.partial(advance, 2))
    both(1, functools.partial(advance, 1))
    advance(3, 0)
    advance(2, 2)
    advance(3, 1)
    advance(2, 3)

    @pl.loop(0, CHUNKS - 2)
    def _(chunk):
        advance(4, chunk)
        advance(3, chunk + 2)

    def net_copy(late, target):
        first, count = NET_GROUPS[late]
        return remote(
            net_out.at[target, pl.ds(first, count)], net_in.at[me, pl.ds(first, count)],
            net_send_sems.at[late], net_recv_sems.at[late], trade=target,
        )

    def send_nets(late):
        for step in range(1, N_TRADE):
            net_copy(late, lax.rem(me + step, N_TRADE)).start()

    def await_nets(late):
        first, count = NET_GROUPS[late]
        whole = remote(
            net_out.at[pl.ds(0, N_TRADE - 1), pl.ds(first, count)],
            net_in.at[pl.ds(0, N_TRADE - 1), pl.ds(first, count)],
            net_send_sems.at[late], net_recv_sems.at[late], trade=me,
        )
        whole.wait_send()
        whole.wait_recv()

    def add_nets(chunk):
        total = jnp.zeros((SETS_DEV, NY * ROWS), F32)
        for sender in range(N_TRADE):
            total = total + net_in[sender, chunk].astype(F32)
        net[pl.ds(pl.multiple_of(chunk * SETS_DEV, SETS_DEV), SETS_DEV), :] = jnp.maximum(total, 0.0)

    def compute(chunk):
        net[...] = jnp.zeros_like(net)
        levels = jnp.concatenate(
            [
                book[chunk, owner // NX, owner % NX, col].reshape(NY * ROWS, LANES)
                for col in range(COLS) for owner in range(NZ * NX)[:: 1 - 2 * (col % 2)]
            ],
            axis=1,
        )

        def strip(tile):
            return pl.ds(pl.multiple_of(tile * TILE, TILE), TILE)

        def price(tile, slot):
            prices[slot] = jnp.dot(levels, sens[:, strip(tile)], preferred_element_type=F32)

        def settle(tile, slot):
            at = strip(tile)
            values = weight[:, at] * softplus(prices[slot] + shift_ref[:, at])
            net[...] += lax.dot_general(
                member[:, at], values.astype(BF16), (((1,), (1,)), ((), ())),
                preferred_element_type=F32,
            )

        tiles = positions // TILE
        price(0, 0)

        @pl.loop(0, tiles // 2 - 1)
        def _(pair):
            price(2 * pair + 1, 1)
            settle(2 * pair, 0)

            @pl.when(chunk < CHUNKS - 2)
            def _():
                advance(4, chunk + 2)

            price(2 * pair + 2, 0)
            settle(2 * pair + 1, 1)

        price(tiles - 1, 1)
        settle(tiles - 2, 0)
        settle(tiles - 1, 1)

        for owner in range(N_TRADE):
            net_out[owner, chunk] = net[owner * SETS_DEV:(owner + 1) * SETS_DEV].astype(BF16)
        net_in[me, chunk] = net_out[me, chunk]

    weight[...] = jnp.where(
        lax.broadcasted_iota(jnp.int32, (1, positions), 1) < live_ref[...],
        principal_ref[...], 0.0,
    )

    @pl.loop(0, positions // TILE)
    def _(tile):
        at = pl.ds(pl.multiple_of(tile * TILE, TILE), TILE)
        labels = lax.broadcasted_iota(jnp.int32, (sets, TILE), 0)
        member[:, at] = (labels == group_ref[:, at]).astype(F32).astype(BF16)

    for by in range(1, NY):
        draw_copy(by, place["y"]).wait_send()
    for part in range(HALVES):
        for step in range(DRAW_STEPS):
            for copy in draw_ring(step, "send", part):
                copy.wait_send()
    for kind in range(2):
        @pl.when(zx < kinds[kind][1])
        def _(kind=kind):
            @pl.loop(1, NZ * NX)
            def _(step):
                root_copy(kind, (zx + step) % (NZ * NX), zx).wait_send()
    for step in range(3):
        for copy in root_ring(step, "send"):
            copy.wait_send()
    for by in range(NY):
        twin_copy(by, core).wait_send()

    def sent(first, last, chunk):
        for part in range(len(PARTS)):
            for step in range(first, last):
                for copy in descriptors(part, step, chunk, "send"):
                    copy.wait_send()

    @pl.loop(0, CHUNKS)
    def _(chunk):
        sent(0, 3, chunk)

    fetch.wait()

    @pl.loop(0, CHUNKS)
    def _(chunk):
        complete(chunk)

        @pl.when(chunk == CHUNKS - 1)
        def _():
            send_nets(0)

        compute(chunk)

    send_nets(1)

    @pl.loop(0, CHUNKS)
    def _(chunk):
        sent(3, STEPS, chunk)

    for late, (first, count) in enumerate(NET_GROUPS):
        await_nets(late)

        @pl.loop(first, first + count)
        def _(chunk):
            add_nets(chunk)

    mean_in[scen] = jnp.zeros(mean_in.shape[1:], F32)
    down = lax.broadcasted_iota(jnp.int32, (SETS_DEV, LANES), 0)
    across = lax.broadcasted_iota(jnp.int32, (SETS_DEV, LANES), 1)
    for date in range(dates):
        strip = jnp.concatenate(
            [
                net[chunk * SETS_DEV:(chunk + 1) * SETS_DEV, y * ROWS + date * part_rows:][:, :part_rows]
                for y in range(NY) for chunk in range(CHUNKS)
            ],
            axis=1,
        )
        out_ref[date] = strip
        sums = jnp.where(down == across, jnp.sum(strip, axis=1, keepdims=True), 0.0)
        mean_in[scen, pl.ds(date, 1), :] = jnp.sum(sums, axis=0, keepdims=True)

    def mean_copy(by, slot):
        return remote(
            mean_in.at[slot], mean_in.at[slot], mean_send.at[by - 1], mean_recv.at[by - 1],
            scen=(scen + by) % scens,
        )

    for by in range(1, scens):
        mean_copy(by, scen).start()

    for by in range(1, scens):
        mean_copy(by, (scen + scens - by) % scens).wait_recv()
        mean_copy(by, scen).wait_send()
    total = jnp.sum(mean_in[...], axis=0) / (scens * NY * span)
    mean_ref[...] = total[:dates, :SETS_DEV]


def exposures(draws, root, sensitivity, pull, shift, principal, group, live):
    dates, scen, _ = draws.shape
    positions = sensitivity.shape[1]
    sets = SETS_DEV * N_TRADE
    span = scen // NY
    vmem = pl.BlockSpec(memory_space=pltpu.VMEM)
    hbm = pl.BlockSpec(memory_space=pl.ANY)
    dma = pltpu.SemaphoreType.DMA
    return pl.pallas_call(
        exposure_kernel,
        out_shape=(
            jax.ShapeDtypeStruct((dates, SETS_DEV, scen), F32),
            jax.ShapeDtypeStruct((dates, SETS_DEV), F32),
        ),
        in_specs=[hbm, hbm, hbm, vmem, vmem, vmem, vmem, vmem],
        out_specs=(vmem, vmem),
        scratch_shapes=[
            pltpu.VMEM((NZ, NX, NY, dates, span, LANES), BF16),
            pltpu.VMEM((2, SLOTS, NY, LANES, LANES), BF16),
            pltpu.VMEM((CHUNKS, NZ, NX, COLS, NY, ROWS, LANES), BF16),
            pltpu.VMEM(sensitivity.shape, BF16),
            pltpu.VMEM((sets, positions), BF16),
            pltpu.VMEM((1, positions), F32),
            pltpu.VMEM((sets, NY * ROWS), F32),
            pltpu.VMEM((2, NY * ROWS, TILE), F32),
            pltpu.VMEM((N_TRADE, CHUNKS, SETS_DEV, NY * ROWS), BF16),
            pltpu.VMEM((N_TRADE, CHUNKS, SETS_DEV, NY * ROWS), BF16),
            pltpu.VMEM((lax.axis_size("scen"), 8, LANES), F32),
            dma((NY - 1,)), dma((NY - 1,)),
            dma((HALVES, dates, DRAW_STEPS, 2)), dma((HALVES, dates, DRAW_STEPS, 2)),
            dma((2, NZ * NX)), dma((2, NZ * NX)),
            dma((3, 2)), dma((3, 2)), dma((NY,)), dma((NY,)),
            dma((CHUNKS, len(PARTS), STEPS, 2)), dma((CHUNKS, len(PARTS), STEPS, 2)),
            dma((3,)), dma, dma((len(NET_GROUPS),)), dma((len(NET_GROUPS),)),
            dma((lax.axis_size("scen") - 1,)), dma((lax.axis_size("scen") - 1,)),
        ],
        compiler_params=pltpu.CompilerParams(
            collective_id=1, has_side_effects=True, vmem_limit_bytes=58 * 2**20
        ),
        cost_estimate=pl.CostEstimate(
            flops=2 * 1024 * positions * (4096 + sets), bytes_accessed=17 << 20, transcendentals=0
        ),
        name="exposures",
    )(
        draws, root, sensitivity, pull.reshape(-1, LANES), shift.reshape(1, -1),
        principal.reshape(1, -1), group.reshape(1, -1), live.reshape(1, 1),
    )


def on_device(
    normal_draws, covariance_root, mean_pullback, sensitivity_tensor,
    moneyness_shift, signed_principal, deal_agreement_group, active_position_number,
):
    exposure, mean = exposures(
        normal_draws, covariance_root, sensitivity_tensor, mean_pullback, moneyness_shift,
        signed_principal, deal_agreement_group, active_position_number,
    )
    return exposure.transpose(0, 2, 1), mean


def solution(mesh):
    in_specs = (
        P(None, "scen", "trade"), P("trade", None), P(), P(None, "trade"),
        P("trade"), P("trade"), P("trade"), P("trade"),
    )
    out_specs = (P(None, "scen", "trade"), P(None, "trade"))
    return jax.shard_map(
        on_device, mesh=mesh, in_specs=in_specs, out_specs=out_specs, check_vma=False
    )
```

```python
import functools
import jax
import jax.numpy as jnp
from jax import lax
from jax.experimental import pallas as pl
from jax.experimental.pallas import tpu as pltpu
from jax.sharding import PartitionSpec as P

F32, BF16 = jnp.float32, jnp.bfloat16
SETS_DEV = 16
NZ, NX, NY = 2, 4, 4
N_TRADE = NZ * NX * NY
CHUNKS = 4
COLS = 4
ROWS = 64
LANES = 128
TILE = 512
HALVES = 2
PARTS = (
    ((0, 3), (0, 32), ("z", "y", "x")),
    ((0, 3), (32, 32), ("z", "x", "y")),
    ((3, 1), (0, 32), ("x", "y", "z")),
    ((3, 1), (32, 32), ("y", "x", "z")),
)
STEPS = 5
DRAW_ORDERS = (("z", "x"), ("x", "z"))
DRAW_STEPS = 3
SLOTS = 10
NET_GROUPS = ((0, CHUNKS - 1), (CHUNKS - 1, 1))


def trade_place():
    me = lax.axis_index("trade")
    return {"z": me // (NX * NY), "x": (me // NY) % NX, "y": me % NY}


def trade_index(place):
    return (place["z"] * NX + place["x"]) * NY + place["y"]


def moved(place, axis, by):
    size = {"z": NZ, "x": NX, "y": NY}[axis]
    return dict(place, **{axis: (place[axis] + by) % size})


def part_steps(place, order):
    have = dict(place)
    steps = []
    for axis in order:
        if axis == "z":
            steps.append(
                (
                    [(dict(have), None, moved(place, "z", 1))],
                    [(dict(have, z=1 - place["z"]), None)],
                )
            )
        else:
            right, left = moved(place, axis, 1), moved(place, axis, 3)
            far = moved(place, axis, 2)
            at = lambda where: dict(have, **{axis: where[axis]})
            steps.append(
                (
                    [(at(place), None, right), (at(place), None, left)],
                    [(at(left), None), (at(right), None)],
                )
            )
            steps.append(
                (
                    [(at(left), 0, right), (at(right), 1, left)],
                    [(at(far), 0), (at(far), 1)],
                )
            )
        have[axis] = None
    return steps


def hand_on(arrivals, sends, pairwise):
    arrivals, sends = list(arrivals), list(sends)
    if pairwise:
        for arrival, send in zip(arrivals, sends):
            arrival.wait_recv()
            send.start()
    else:
        for arrival in arrivals:
            arrival.wait_recv()
        for send in sends:
            send.start()


def softplus(a):
    return jnp.maximum(a, 0.0) + jnp.log(1.0 + jnp.exp(-jnp.abs(a)))


def factor_block(col, owner):
    return 8 * col + (owner if col % 2 == 0 else 7 - owner)


def column_home(col):
    return {3: (0, 0), 0: (0, 8), 2: (1, 0), 1: (1, 6)}[col]


def exposure_kernel(
    draws_hbm, root_hbm, sens_hbm, pull_ref, shift_ref, principal_ref, group_ref, live_ref,
    out_ref, mean_ref,
    draws, root, book, sens, member, weight, net, prices, net_out, net_in, mean_in,
    draw_send, draw_recv, draw_ring_send, draw_ring_recv,
    root_send, root_recv, root_ring_send, root_ring_recv, twin_send, twin_recv,
    send_sems, recv_sems, own_sems, sens_sem, net_send_sems, net_recv_sems,
    mean_send, mean_recv,
):
    place = trade_place()
    me = trade_index(place)
    zx = place["z"] * NX + place["x"]
    scen = lax.axis_index("scen")
    scens = lax.axis_size("scen")
    core = scen % 2
    twin = scen + 1 - 2 * core
    positions = sens.shape[1]
    sets = member.shape[0]
    span = draws_hbm.shape[1] // NY

    def remote(src, dst, send, recv, **target):
        return pltpu.make_async_remote_copy(
            src_ref=src, dst_ref=dst, send_sem=send, recv_sem=recv,
            device_id=target, device_id_type=pl.DeviceIdType.MESH,
        )

    barrier = pltpu.get_barrier_semaphore()

    greeted = [trade_index(moved(place, "y", by)) for by in range(1, NY)]
    greeted += [lax.rem(me + step * NY, N_TRADE) for step in range(1, NZ * NX)]
    for target in greeted:
        pl.semaphore_signal(
            barrier, inc=1, device_id={"trade": target}, device_id_type=pl.DeviceIdType.MESH,
        )

    @pl.loop(1, scens)
    def _(step):
        pl.semaphore_signal(
            barrier, inc=1, device_id={"scen": (scen + step) % scens},
            device_id_type=pl.DeviceIdType.MESH,
        )

    pl.semaphore_wait(barrier, len(greeted) + scens - 1)

    def draw_rows(y):
        return draws_hbm.at[:, pl.ds(y * span, span), :]

    def draw_copy(by, source):
        return remote(
            draw_rows((place["y"] + by) % NY), draws.at[place["z"], place["x"], source],
            draw_send.at[by - 1], draw_recv.at[by - 1],
            trade=trade_index(moved(place, "y", by)),
        )

    own_draws = pltpu.make_async_copy(
        draw_rows(place["y"]), draws.at[place["z"], place["x"], place["y"]], own_sems.at[0]
    )
    own_draws.start()
    for by in range(1, NY):
        draw_copy(by, place["y"]).start()

    high_count, low_count = 8 - 2 * core, 2 + 2 * core
    kinds = ((3 - core, high_count, 0), (core, low_count, high_count))

    def root_block(kind, owner):
        col = kinds[kind][0]
        block = 8 * col + jnp.where(col % 2 == 0, owner, 7 - owner)
        return root_hbm.at[:, pl.ds(pl.multiple_of(block * LANES, LANES), LANES)]

    def root_slot(kind, source):
        return root.at[core, kinds[kind][2] + source, place["y"]]

    def root_copy(kind, owner, source):
        return remote(
            root_block(kind, owner), root_slot(kind, source),
            root_send.at[kind, owner], root_recv.at[kind, source],
            trade=owner * NY + place["y"],
        )

    def own_root(kind):
        return pltpu.make_async_copy(root_block(kind, zx), root_slot(kind, zx), own_sems.at[1 + kind])

    for kind in range(2):
        @pl.when(zx < kinds[kind][1])
        def _(kind=kind):
            own_root(kind).start()

            @pl.loop(1, NZ * NX)
            def _(step):
                root_copy(kind, (zx + step) % (NZ * NX), zx).start()

    fetch = pltpu.make_async_copy(sens_hbm, sens, sens_sem)
    fetch.start()

    draw_plans = [part_steps(place, order) for order in DRAW_ORDERS]

    def draw_ring(step, kind, part, only=None):
        for date, plan in reversed(list(enumerate(draw_plans))):
            if only is not None and date != only:
                continue
            sends, recvs = plan[step]
            for way in range(len(sends)):
                coords, half = (sends if kind == "send" else recvs)[way][:2]
                target = sends[way][2]
                rows = span // HALVES
                row = part * rows
                if half is not None:
                    rows = rows // 2
                    row = row + half * rows
                pick = [slice(None) if coords[a] is None else coords[a] for a in "zx"]
                ref = draws.at[pick[0], pick[1], :, date, pl.ds(row, rows), :]
                yield remote(
                    ref, ref, draw_ring_send.at[part, date, step, way],
                    draw_ring_recv.at[part, date, step, way],
                    trade=trade_index(target),
                )

    def root_ring(step, kind):
        y = place["y"]
        right, left = moved(place, "y", 1), moved(place, "y", 3)
        far = (y + 2) % NY
        half = SLOTS // 2
        if step < 2:
            at = {"send": (y, y), "recv": (left["y"], right["y"])}[kind]
        else:
            at = {"send": (left["y"], right["y"]), "recv": (far, far)}[kind]
        refs = [
            root.at[core, pl.ds(half * (way if step != 1 else 1 - way), half), a]
            for way, a in enumerate(at)
        ]
        for way, target in enumerate((right, left)):
            yield remote(
                refs[way], refs[way], root_ring_send.at[step, way], root_ring_recv.at[step, way],
                trade=trade_index(target),
            )

    def twin_copy(by, from_core):
        ref = root.at[from_core, :, (place["y"] + by) % NY]
        return remote(ref, ref, twin_send.at[by], twin_recv.at[by], scen=twin)

    own_draws.wait()
    for by in range(1, NY):
        draw_copy(by, (place["y"] + NY - by) % NY).wait_recv()
    def draw_start(step, part):
        for copy in draw_ring(step, "send", part):
            copy.start()

    def draw_advance(step, part):
        for date, plan in reversed(list(enumerate(draw_plans))):
            hand_on(
                draw_ring(step - 1, "recv", part, date), draw_ring(step, "send", part, date),
                plan[step][0][0][1] is not None,
            )

    def draw_arrived(step, part):
        for copy in draw_ring(step, "recv", part):
            copy.wait_recv()

    for part in range(HALVES):
        draw_start(0, part)

    for kind in range(2):
        @pl.when(zx < kinds[kind][1])
        def _(kind=kind):
            own_root(kind).wait()

        @pl.loop(0, NZ * NX)
        def _(source, kind=kind):
            @pl.when(jnp.logical_and(source < kinds[kind][1], source != zx))
            def _():
                root_copy(kind, zx, source).wait_recv()
    for step in range(2):
        for copy in root_ring(step, "send"):
            copy.start()
    twin_copy(0, core).start()

    for part in range(HALVES):
        draw_advance(1, part)

    hand_on(root_ring(0, "recv"), root_ring(2, "send"), True)
    for copy in root_ring(1, "recv"):
        copy.wait_recv()
    twin_copy(1, core).start()
    twin_copy(3, core).start()

    for part in range(HALVES):
        draw_advance(2, part)

    for copy in root_ring(2, "recv"):
        copy.wait_recv()
    twin_copy(2, core).start()

    for by in range(NY):
        twin_copy(by, 1 - core).wait_recv()

    dates = draws.shape[3]
    part_rows = span // CHUNKS

    def make_levels(part):
        rows = span // HALVES
        for col in range(COLS):
            home, slot = column_home(col)
            sources = [(s, y) for s in range(2 * (col + 1)) for y in range(NY)]
            left = jnp.concatenate(
                [
                    draws[s // NX, s % NX, y, :, pl.ds(part * rows, rows), :].reshape(dates * rows, LANES)
                    for s, y in sources
                ],
                axis=1,
            )
            right = jnp.concatenate([root[home, slot + s, y] for s, y in sources], axis=0)
            shocks = jnp.dot(left, right, preferred_element_type=F32)
            pull = pull_ref[pl.ds(factor_block(col, zx), 1), :]
            state = jnp.zeros((rows, LANES), F32)
            for date in range(dates):
                state = pull * state + shocks[date * rows:(date + 1) * rows]
                levels = state.astype(BF16)
                for chunk in range(CHUNKS // HALVES):
                    book[
                        part * (CHUNKS // HALVES) + chunk, place["z"], place["x"], col, place["y"],
                        pl.ds(date * part_rows, part_rows), :,
                    ] = levels[chunk * part_rows:(chunk + 1) * part_rows]

    plans = [part_steps(place, order) for _, _, order in PARTS]

    def view(part, chunk, coords, half):
        (col, cols), (row, rows), _ = PARTS[part]
        if half is not None:
            rows = rows // 2
            row = row + half * rows
        pick = [slice(None) if coords[a] is None else coords[a] for a in "zxy"]
        return book.at[chunk, pick[0], pick[1], pl.ds(col, cols), pick[2], pl.ds(row, rows), :]

    def descriptors(part, step, chunk, kind):
        sends, recvs = plans[part][step]
        for way in range(len(sends)):
            if kind == "send":
                coords, half, target = sends[way]
            else:
                coords, half = recvs[way]
                target = place
            ref = view(part, chunk, coords, half)
            yield remote(
                ref, ref, send_sems.at[chunk, part, step, way], recv_sems.at[chunk, part, step, way],
                trade=trade_index(target),
            )

    def start(chunk):
        for part in range(len(PARTS)):
            for copy in descriptors(part, 0, chunk, "send"):
                copy.start()

    def advance(step, chunk):
        for part in range(len(PARTS)):
            hand_on(
                descriptors(part, step - 1, chunk, "recv"), descriptors(part, step, chunk, "send"),
                plans[part][step][0][0][1] is not None,
            )

    def complete(chunk):
        for part in range(len(PARTS)):
            for copy in descriptors(part, STEPS - 1, chunk, "recv"):
                copy.wait_recv()

    half_chunks = CHUNKS // HALVES

    def both(part, act):
        @pl.loop(part * half_chunks, (part + 1) * half_chunks)
        def _(chunk):
            act(chunk)

    draw_arrived(2, 0)
    make_levels(0)
    both(0, start)
    both(0, functools.partial(advance, 1))
    draw_arrived(2, 1)
    make_levels(1)
    both(1, start)
    both(0, functools.partial(advance, 2))
    both(1, functools.partial(advance, 1))
    advance(3, 0)
    advance(2, 2)
    advance(3, 1)
    advance(2, 3)

    @pl.loop(0, CHUNKS - 2)
    def _(chunk):
        advance(4, chunk)
        advance(3, chunk + 2)

    def net_copy(late, target):
        first, count = NET_GROUPS[late]
        return remote(
            net_out.at[target, pl.ds(first, count)], net_in.at[me, pl.ds(first, count)],
            net_send_sems.at[late], net_recv_sems.at[late], trade=target,
        )

    def send_nets(late):
        for step in range(1, N_TRADE):
            net_copy(late, lax.rem(me + step, N_TRADE)).start()

    def await_nets(late):
        first, count = NET_GROUPS[late]
        whole = remote(
            net_out.at[pl.ds(0, N_TRADE - 1), pl.ds(first, count)],
            net_in.at[pl.ds(0, N_TRADE - 1), pl.ds(first, count)],
            net_send_sems.at[late], net_recv_sems.at[late], trade=me,
        )
        whole.wait_send()
        whole.wait_recv()

    def add_nets(chunk):
        total = jnp.zeros((SETS_DEV, NY * ROWS), F32)
        for sender in range(N_TRADE):
            total = total + net_in[sender, chunk].astype(F32)
        net[pl.ds(pl.multiple_of(chunk * SETS_DEV, SETS_DEV), SETS_DEV), :] = total

    def compute(chunk):
        net[...] = jnp.zeros_like(net)
        levels = jnp.concatenate(
            [
                book[chunk, owner // NX, owner % NX, col].reshape(NY * ROWS, LANES)
                for col in range(COLS) for owner in range(NZ * NX)[:: 1 - 2 * (col % 2)]
            ],
            axis=1,
        )

        def strip(tile):
            return pl.ds(pl.multiple_of(tile * TILE, TILE), TILE)

        def price(tile, slot):
            prices[slot] = jnp.dot(levels, sens[:, strip(tile)], preferred_element_type=F32)

        def settle(tile, slot):
            at = strip(tile)
            values = weight[:, at] * softplus(prices[slot] + shift_ref[:, at])
            net[...] += lax.dot_general(
                member[:, at], values.astype(BF16), (((1,), (1,)), ((), ())),
                preferred_element_type=F32,
            )

        tiles = positions // TILE
        price(0, 0)

        @pl.loop(0, tiles // 2 - 1)
        def _(pair):
            price(2 * pair + 1, 1)
            settle(2 * pair, 0)

            @pl.when(chunk < CHUNKS - 2)
            def _():
                advance(4, chunk + 2)

            price(2 * pair + 2, 0)
            settle(2 * pair + 1, 1)

        price(tiles - 1, 1)
        settle(tiles - 2, 0)
        settle(tiles - 1, 1)

        for owner in range(N_TRADE):
            net_out[owner, chunk] = net[owner * SETS_DEV:(owner + 1) * SETS_DEV].astype(BF16)
        net_in[me, chunk] = net_out[me, chunk]

    weight[...] = jnp.where(
        lax.broadcasted_iota(jnp.int32, (1, positions), 1) < live_ref[...],
        principal_ref[...], 0.0,
    )

    @pl.loop(0, positions // TILE)
    def _(tile):
        at = pl.ds(pl.multiple_of(tile * TILE, TILE), TILE)
        labels = lax.broadcasted_iota(jnp.int32, (sets, TILE), 0)
        member[:, at] = (labels == group_ref[:, at]).astype(F32).astype(BF16)

    for by in range(1, NY):
        draw_copy(by, place["y"]).wait_send()
    for part in range(HALVES):
        for step in range(DRAW_STEPS):
            for copy in draw_ring(step, "send", part):
                copy.wait_send()
    for kind in range(2):
        @pl.when(zx < kinds[kind][1])
        def _(kind=kind):
            @pl.loop(1, NZ * NX)
            def _(step):
                root_copy(kind, (zx + step) % (NZ * NX), zx).wait_send()
    for step in range(3):
        for copy in root_ring(step, "send"):
            copy.wait_send()
    for by in range(NY):
        twin_copy(by, core).wait_send()

    def sent(first, last, chunk):
        for part in range(len(PARTS)):
            for step in range(first, last):
                for copy in descriptors(part, step, chunk, "send"):
                    copy.wait_send()

    @pl.loop(0, CHUNKS)
    def _(chunk):
        sent(0, 3, chunk)

    fetch.wait()

    @pl.loop(0, CHUNKS)
    def _(chunk):
        complete(chunk)

        @pl.when(chunk == CHUNKS - 1)
        def _():
            send_nets(0)

        compute(chunk)

    send_nets(1)

    @pl.loop(0, CHUNKS)
    def _(chunk):
        sent(3, STEPS, chunk)

    for late, (first, count) in enumerate(NET_GROUPS):
        await_nets(late)

        @pl.loop(first, first + count)
        def _(chunk):
            add_nets(chunk)

    mean_in[scen] = jnp.zeros(mean_in.shape[1:], F32)
    down = lax.broadcasted_iota(jnp.int32, (SETS_DEV, LANES), 0)
    across = lax.broadcasted_iota(jnp.int32, (SETS_DEV, LANES), 1)
    for date in range(dates):
        strip = jnp.concatenate(
            [
                net[chunk * SETS_DEV:(chunk + 1) * SETS_DEV, y * ROWS + date * part_rows:][:, :part_rows]
                for y in range(NY) for chunk in range(CHUNKS)
            ],
            axis=1,
        )
        out_ref[date] = strip
        strip = jnp.maximum(strip, 0.0)
        sums = jnp.where(down == across, jnp.sum(strip, axis=1, keepdims=True), 0.0)
        mean_in[scen, pl.ds(date, 1), :] = jnp.sum(sums, axis=0, keepdims=True)

    def mean_copy(by, slot):
        return remote(
            mean_in.at[slot], mean_in.at[slot], mean_send.at[by - 1], mean_recv.at[by - 1],
            scen=(scen + by) % scens,
        )

    for by in range(1, scens):
        mean_copy(by, scen).start()

    for by in range(1, scens):
        mean_copy(by, (scen + scens - by) % scens).wait_recv()
        mean_copy(by, scen).wait_send()
    total = jnp.sum(mean_in[...], axis=0)
    mean_ref[...] = total[:dates, :SETS_DEV]


def exposures(draws, root, sensitivity, pull, shift, principal, group, live):
    dates, scen, _ = draws.shape
    positions = sensitivity.shape[1]
    sets = SETS_DEV * N_TRADE
    span = scen // NY
    vmem = pl.BlockSpec(memory_space=pltpu.VMEM)
    hbm = pl.BlockSpec(memory_space=pl.ANY)
    dma = pltpu.SemaphoreType.DMA
    return pl.pallas_call(
        exposure_kernel,
        out_shape=(
            jax.ShapeDtypeStruct((dates, SETS_DEV, scen), F32),
            jax.ShapeDtypeStruct((dates, SETS_DEV), F32),
        ),
        in_specs=[hbm, hbm, hbm, vmem, vmem, vmem, vmem, vmem],
        out_specs=(vmem, vmem),
        scratch_shapes=[
            pltpu.VMEM((NZ, NX, NY, dates, span, LANES), BF16),
            pltpu.VMEM((2, SLOTS, NY, LANES, LANES), BF16),
            pltpu.VMEM((CHUNKS, NZ, NX, COLS, NY, ROWS, LANES), BF16),
            pltpu.VMEM(sensitivity.shape, BF16),
            pltpu.VMEM((sets, positions), BF16),
            pltpu.VMEM((1, positions), F32),
            pltpu.VMEM((sets, NY * ROWS), F32),
            pltpu.VMEM((2, NY * ROWS, TILE), F32),
            pltpu.VMEM((N_TRADE, CHUNKS, SETS_DEV, NY * ROWS), BF16),
            pltpu.VMEM((N_TRADE, CHUNKS, SETS_DEV, NY * ROWS), BF16),
            pltpu.VMEM((lax.axis_size("scen"), 8, LANES), F32),
            dma((NY - 1,)), dma((NY - 1,)),
            dma((HALVES, dates, DRAW_STEPS, 2)), dma((HALVES, dates, DRAW_STEPS, 2)),
            dma((2, NZ * NX)), dma((2, NZ * NX)),
            dma((3, 2)), dma((3, 2)), dma((NY,)), dma((NY,)),
            dma((CHUNKS, len(PARTS), STEPS, 2)), dma((CHUNKS, len(PARTS), STEPS, 2)),
            dma((3,)), dma, dma((len(NET_GROUPS),)), dma((len(NET_GROUPS),)),
            dma((lax.axis_size("scen") - 1,)), dma((lax.axis_size("scen") - 1,)),
        ],
        compiler_params=pltpu.CompilerParams(
            collective_id=1, has_side_effects=True, vmem_limit_bytes=58 * 2**20
        ),
        cost_estimate=pl.CostEstimate(
            flops=2 * 1024 * positions * (4096 + sets), bytes_accessed=17 << 20, transcendentals=0
        ),
        name="exposures",
    )(
        draws, root, sensitivity, pull.reshape(-1, LANES), shift.reshape(1, -1),
        principal.reshape(1, -1), group.reshape(1, -1), live.reshape(1, 1),
    )


def on_device(
    normal_draws, covariance_root, mean_pullback, sensitivity_tensor,
    moneyness_shift, signed_principal, deal_agreement_group, active_position_number,
):
    nets, sums = exposures(
        normal_draws, covariance_root, sensitivity_tensor, mean_pullback, moneyness_shift,
        signed_principal, deal_agreement_group, active_position_number,
    )
    exposure = jnp.maximum(nets, 0.0).transpose(0, 2, 1)
    return exposure, sums / (normal_draws.shape[1] * lax.axis_size("scen"))


def solution(mesh):
    in_specs = (
        P(None, "scen", "trade"), P("trade", None), P(), P(None, "trade"),
        P("trade"), P("trade"), P("trade"), P("trade"),
    )
    out_specs = (P(None, "scen", "trade"), P(None, "trade"))
    return jax.shard_map(
        on_device, mesh=mesh, in_specs=in_specs, out_specs=out_specs, check_vma=False
    )
```
